32 devices in a mesh: groups: 2 (over x), tile: 16 (over z, y, core).
Axes of the slice: x: 2, y: 2, z: 4, core: 2. Of those that a mesh axis runs over, the one named last changes fastest.
Arguments:
- features: bfloat16 [128, 256, 2048], P(('groups', 'tile')), parts along dimension 0, may hold values from -0.5 to 0.5
- gauge_offset: int32 [128, 384], P(('groups', 'tile')), parts along dimension 0, may hold values from 0 to 248
- gauge_count: int32 [128], P(('groups', 'tile')), parts along dimension 0, may hold values from 1 to 384, as said below
- gauge_resid: bfloat16 [128, 384], P(('groups', 'tile')), parts along dimension 0, may hold values from -6 to 6
- damping: float32 [4096], P('groups'), parts along dimension 0, may hold values from 0.5 to 2
Outputs:
- panel_factor: float32 [512, 256], P('groups'), parts along dimension 0
- lower_trail: float32 [3584, 256], P(('groups', 'tile')), parts along dimension 0
- schur: float32 [3584, 1792], P(('groups', 'tile')), parts along dimension 0
- panel_rhs: float32 [512], P('groups'), parts along dimension 0
- trail_rhs: float32 [3584], P(('groups', 'tile')), parts along dimension 0
The draws below stay inside these ranges and needn't reach their ends.
There are 2 independent parts, one for each index of `groups`. The reference program is written for one: setup_inputs(seed, part) draws one part's arguments, and reference() takes and returns one part's arrays. A program takes and returns all parts, laid end to end along the dimension named above; each array names one. Nothing has to cross between parts.
Inputs may be any that keep to these rules, and one draw needn't show every extreme that they name: `gauge_count`: the counts of the 4 tiles of one device sum to at most 768; in every draw some device reaches that sum, and some tile has 384 live gauges.
All inputs are finite; a program needn't handle non-finite values.
Results may differ from the reference program's by a relative error of at most 0.0033.
Values sent between devices are 32-bit elements; how exact they have to be, the bound alone decides.
No kernel may reach another device: no remote copies, remote signals or barrier semaphores. Data moves between devices by JAX's collectives and lax.ppermute only.
A program may use at most 128 MiB of HBM per device.

```python
import math
import jax
import jax.numpy as jnp
from jax import lax

P_SIZE = 2048
PB = 256
W = 256
LWIN = 8
GMAX = 384
TILES_DEV = 4
TILES = 64
SLOTS = 24576


def draw_gauge_count(key, part):
    key = jax.random.fold_in(key, 11)
    devices_all = TILES // TILES_DEV
    most_load = TILES_DEV * GMAX // 2
    other_max = (most_load - GMAX) // (TILES_DEV - 1)
    key_heavy, key_rest, key_pick, key_order = jax.random.split(key, 4)
    heavy = jax.random.randint(key_heavy, (devices_all, 1), 1, GMAX + 1)
    others = jax.random.randint(key_rest, (devices_all, TILES_DEV - 1), 1, other_max + 1)
    counts = jnp.concatenate([heavy, others], axis=1)
    spare = most_load - GMAX - (TILES_DEV - 1) * other_max
    extra = (jnp.arange(TILES_DEV - 1) < spare).astype(jnp.int32)
    forced = jnp.concatenate([jnp.array([GMAX], jnp.int32), other_max + extra])
    chosen = jax.random.randint(key_pick, (), 0, devices_all)
    counts = jnp.where(jnp.arange(devices_all)[:, None] == chosen, forced[None, :], counts)
    scores = jax.random.randint(key_order, (devices_all, TILES_DEV), 0, 2 ** 20) * TILES_DEV + jnp.arange(TILES_DEV)[None, :]
    order = jnp.argsort(scores, axis=1)
    counts = jnp.take_along_axis(counts, order, axis=1)
    return counts.reshape(TILES).astype(jnp.int32)


def place_ends(entries, own_key, low, high):
    extent = entries.shape
    spot = [jax.random.randint(jax.random.fold_in(own_key, axis), (), 0, extent[axis]) for axis in range(len(extent))]
    entries = entries.at[tuple(spot)].set(low)
    longest = extent.index(max(extent))
    spot[longest] = (spot[longest] + 1) % extent[longest]
    return entries.at[tuple(spot)].set(high)


def levels(own_key, extent, cuts, low, top_value):
    factor_of, own = 1.0, jax.random.fold_in(own_key, 6)
    for dim, blocks in cuts:
        steps = jnp.exp(jax.random.uniform(jax.random.fold_in(own, dim), (blocks,), jnp.float32, low / len(cuts), top_value / len(cuts)))
        factor_of = factor_of * jnp.repeat(steps, extent[dim] // blocks).reshape([-1 if axis == dim else 1 for axis in range(len(extent))])
    return factor_of


def centred(key, extent, deviation, limit, shards=(), kind=jnp.bfloat16):
    drawn = deviation * jax.random.normal(key, extent, jnp.float32)
    if shards:
        drawn = drawn * levels(key, extent, shards, -0.22, 0.18)
    return jnp.clip(drawn, -limit, limit).astype(kind)


def setup_inputs(seed: int = 0, part: int = 0) -> dict:
    keys = jax.random.split(jax.random.key(seed), 6)
    part_splits = jax.random.split(jax.random.fold_in(keys[5], part), 6)
    features = centred(part_splits[0], (TILES, W, P_SIZE), ((SLOTS // 32) ** -0.5), 0.5, ((0, 16),))
    gauge_offset = place_ends(jax.random.randint(part_splits[1], (TILES, GMAX), 0, W - LWIN + 1), jax.random.fold_in(part_splits[1], 1), 0, W - LWIN).astype(jnp.int32)
    gauge_count = draw_gauge_count(jax.random.fold_in(jax.random.fold_in(keys[5], part), 71), part)
    gauge_resid = centred(part_splits[3], (TILES, GMAX), 1.0, 6.0, ((0, 16),))
    damping = jnp.clip(jnp.exp(jax.random.uniform(part_splits[4], (P_SIZE,), jnp.float32, math.log(0.5), math.log(2.0))), 0.5, 2.0)
    return dict(features=features, gauge_offset=gauge_offset, gauge_count=gauge_count, gauge_resid=gauge_resid, damping=damping)


def reference(features, gauge_offset, gauge_count, gauge_resid, damping):
    slot_ids = lax.broadcasted_iota(jnp.int32, (TILES, GMAX), 1)
    live = slot_ids < gauge_count[:, None]
    sample_ids = lax.broadcasted_iota(jnp.int32, (GMAX, W), 1)

    def one_tile(packed):
        feats, offs, alive = packed
        inside = (sample_ids >= offs[:, None]) & (sample_ids < offs[:, None] + LWIN) & alive[:, None]
        window = jnp.where(inside, 1.0 / LWIN, 0.0).astype(jnp.bfloat16)
        return jnp.dot(window.astype(jnp.float32), feats.astype(jnp.float32), preferred_element_type=jnp.float32).astype(jnp.bfloat16)
    jac = lax.map(one_tile, (features, gauge_offset, live)).reshape(SLOTS, P_SIZE)
    resid = jnp.where(live, gauge_resid, jnp.zeros_like(gauge_resid)).reshape(SLOTS)
    jac_wide = jac.astype(jnp.float32)
    grad = jnp.dot(resid.astype(jnp.float32), jac_wide, precision=lax.Precision.HIGHEST)
    normal = jnp.dot(jac_wide.T, jac_wide, precision=lax.Precision.HIGHEST) + jnp.diag(damping)
    blocks = normal.reshape(PB, 8, P_SIZE)
    panel_rows = blocks[:, 0, :]
    trail_rows = blocks[:, 1:, :].reshape(P_SIZE - PB, P_SIZE)
    n11 = panel_rows.reshape(PB, PB, 8)[:, :, 0]
    n21 = trail_rows.reshape(P_SIZE - PB, PB, 8)[:, :, 0]
    n22 = trail_rows.reshape(P_SIZE - PB, PB, 8)[:, :, 1:].reshape(P_SIZE - PB, P_SIZE - PB)
    grad_blocks = grad.reshape(PB, 8)
    first_part = grad_blocks[:, 0]
    second_part = grad_blocks[:, 1:].reshape(P_SIZE - PB)
    panel_factor = jnp.linalg.cholesky(n11)
    lower_trail = lax.linalg.triangular_solve(panel_factor, n21, left_side=False, lower=True, transpose_a=True)
    schur = n22 - jnp.dot(lower_trail, lower_trail.T, precision=lax.Precision.HIGHEST)
    panel_rhs = lax.linalg.triangular_solve(panel_factor, first_part[:, None], left_side=True, lower=True)[:, 0]
    trail_rhs = second_part - jnp.dot(lower_trail, panel_rhs, precision=lax.Precision.HIGHEST)
    return (panel_factor, lower_trail, schur, panel_rhs, trail_rhs)
```

```python
import functools

import jax
import jax.numpy as jnp
from jax import lax
from jax.experimental import pallas as pl
from jax.experimental.pallas import tpu as pltpu
from jax.sharding import PartitionSpec as P

LWIN = 8
STRIDE = 8
BLK = 256
EXACT = lax.Precision.HIGHEST
VMEM_LIMIT = 56 * 2**20

SMEM_SPEC = pl.BlockSpec(memory_space=pltpu.SMEM)
VMEM_SPEC = pl.BlockSpec(memory_space=pltpu.VMEM)
NT = (((1,), (1,)), ((), ()))


def f32(*shape):
    return jax.ShapeDtypeStruct(shape, jnp.float32)


def bf16(*shape):
    return jax.ShapeDtypeStruct(shape, jnp.bfloat16)


def dot_nt(a, b, precision=None):
    return lax.dot_general(a, b, NT, precision=precision, preferred_element_type=jnp.float32)


def call(kernel, ins, out_shape, scratch=(), flops=0, moved=0):
    return pl.pallas_call(
        kernel,
        out_shape=out_shape,
        in_specs=[SMEM_SPEC if x.dtype == jnp.int32 and x.ndim == 1 else VMEM_SPEC for x in ins],
        out_specs=jax.tree.map(lambda _: VMEM_SPEC, out_shape),
        scratch_shapes=list(scratch),
        compiler_params=pltpu.CompilerParams(vmem_limit_bytes=VMEM_LIMIT),
        cost_estimate=pl.CostEstimate(flops=flops, bytes_accessed=moved, transcendentals=0),
    )(*ins)


def owner_of(m, order):
    last = len(order) - 1
    return sum(((m >> (last - k)) & 1) << bit for k, bit in enumerate(order))


def front_kernel(order, me_ref, count_ref, offset_ref, resid_ref, feat_ref, sent_ref, kept_ref, pan_sent_ref, jt_ref, jp_ref, r_ref, n11_ref):
    tiles, slots = offset_ref.shape
    depth, params = feat_ref.shape
    samples = depth // tiles
    cap = jp_ref.shape[1]
    panel = jp_ref.shape[0]
    trail = params - panel
    core = me_ref[0] & 1
    lane = lax.broadcasted_iota(jnp.int32, (8, cap), 1)
    start = jnp.full((8, cap), -depth, jnp.int32)
    resid = jnp.zeros((8, cap), jnp.float32)
    before = jnp.int32(0)
    for t in range(tiles):
        count = count_ref[t]
        live = (lane >= before) & (lane < before + count)
        offs = jnp.concatenate([offset_ref[t : t + 1, :], jnp.zeros((1, cap - slots), jnp.int32)], axis=1)
        offs = pltpu.roll(jnp.broadcast_to(offs, (8, cap)), before, 1)
        res = jnp.concatenate([resid_ref[t : t + 1, :].astype(jnp.float32), jnp.zeros((1, cap - slots), jnp.float32)], axis=1)
        res = pltpu.roll(jnp.broadcast_to(res, (8, cap)), before, 1)
        start = jnp.where(live, offs + t * samples, start)
        resid = jnp.where(live, res, resid)
        before = before + count
    first = lax.broadcasted_iota(jnp.int32, (8, cap), 0) == 0
    resid = jnp.where(first, resid, 0.0).astype(jnp.bfloat16)
    r_ref[...] = jnp.concatenate([resid, jnp.zeros((8, cap), jnp.bfloat16)], axis=0)
    after = lax.broadcasted_iota(jnp.int32, (depth, cap), 0) - start[0:1, :]
    window = jnp.where((after >= 0) & (after < LWIN), 1.0 / LWIN, 0.0).astype(jnp.bfloat16)
    pan_b = BLK // STRIDE
    row = lax.broadcasted_iota(jnp.int32, (BLK, BLK), 0)
    col = lax.broadcasted_iota(jnp.int32, (BLK, BLK), 1)
    rest = row - pan_b
    source = jnp.where(row < pan_b, row * STRIDE, rest + 1 + ((rest * 9363) >> 16))
    pick = jnp.where(source == col, 1.0, 0.0).astype(jnp.bfloat16)
    trail_b = BLK - pan_b
    for b in range(params // BLK):
        turned = dot_nt(pick, feat_ref[:, b * BLK : (b + 1) * BLK]).astype(jnp.bfloat16)
        jac = jnp.dot(turned, window, preferred_element_type=jnp.float32).astype(jnp.bfloat16)
        jp_ref[b * pan_b : (b + 1) * pan_b, :] = jac[:pan_b]
        jt_ref[b * trail_b : (b + 1) * trail_b, :] = jac[pan_b:]
        if trail + (b + 1) * trail_b <= jt_ref.shape[0]:
            jt_ref[trail + b * trail_b : trail + (b + 1) * trail_b, :] = jac[pan_b:]
    jp = jp_ref[...]
    n11_ref[:panel, :] = dot_nt(jp, jp)
    n11_ref[panel:, :] = dot_nt(r_ref[...], jp)
    half = kept_ref.shape[0]
    kept_ref[...] = n11_ref[pl.ds(pl.multiple_of(core * half, 8), half), :]
    sent_ref[...] = n11_ref[pl.ds(pl.multiple_of((1 - core) * half, 8), half), :]
    panel_part(order, 1 - core, jt_ref, jp_ref, pan_sent_ref)


def panel_part(order, core, jt_ref, jp_ref, out_ref):
    own = out_ref.shape[1]

    def step(m, carry):
        owner = owner_of(m, order) + core
        rows = jt_ref[pl.ds(pl.multiple_of(owner * own, 16), own), :]
        out_ref[m] = dot_nt(rows, jp_ref[...])
        return carry

    lax.fori_loop(0, out_ref.shape[0], step, 0)


def trail_part(orders, core, jt_ref, r_ref, out_refs):
    own, wide = out_refs[0].shape[1:]
    last = len(out_refs) - 1
    extra = r_ref.shape[0]

    def step(m, carry):
        for q, out_ref in enumerate(out_refs):
            base = (owner_of(m, orders[q]) + core) * own
            rows = jt_ref[pl.ds(pl.multiple_of(base, 16), own), :]
            if q < last:
                others = jt_ref[pl.ds(pl.multiple_of(base + q * wide, 16), wide), :]
            else:
                others = jt_ref[pl.ds(pl.multiple_of(base + q * wide, 16), wide - extra), :]
                others = jnp.concatenate([others, r_ref[...]], axis=0)
            out_ref[m] = dot_nt(rows, others)
        return carry

    lax.fori_loop(0, out_refs[0].shape[0], step, 0)


def sent_kernel(orders, order, me_ref, jt_ref, jp_ref, r_ref, pan_ref, *out_refs):
    core = me_ref[0] & 1
    panel_part(order, core, jt_ref, jp_ref, pan_ref)
    trail_part(orders, 1 - core, jt_ref, r_ref, out_refs)


def kept_kernel(orders, me_ref, jt_ref, r_ref, *out_refs):
    trail_part(orders, me_ref[0] & 1, jt_ref, r_ref, out_refs)


def swap(x, axis, bit):
    n = lax.axis_size(axis)
    return lax.ppermute(x, axis, [(i, i ^ (1 << bit)) for i in range(n)])


def halve(kept, got, me, order, axis):
    for bit in order:
        mine = (me >> bit) & 1
        size = kept.shape[0] // 2
        kept = kept.reshape((2, size) + kept.shape[1:])
        got = got.reshape(kept.shape)

        def part(which, kept=kept, got=got):
            return lax.dynamic_index_in_dim(kept, which, 0, False) + lax.dynamic_index_in_dim(got, which, 0, False)

        got = swap(part(1 - mine), axis, bit)
        kept = part(mine)
    return (kept + got)[0]


def mirror(chunks, own, count):
    wide = chunks[0].shape[1]

    def kernel(*refs):
        ins, outs, g_ref, turned_ref = refs[: len(chunks)], refs[len(chunks) : -2], refs[-2], refs[-1]
        for q, ref in enumerate(ins):
            turned_ref[q * wide : (q + 1) * wide, :] = ref[...].T
        for k, out in enumerate(outs):
            out[...] = turned_ref[(k + 1) * own : (k + 2) * own, :]
        g_ref[...] = turned_ref[(count + 2) * own : (count + 2) * own + 8, :]

    total = wide * len(chunks)
    return call(kernel, chunks, [f32(own, own)] * count + [f32(8, own)], [pltpu.VMEM((total, own), jnp.float32)], 0, 8 * total * own)


def factor_block(a):
    size = a.shape[0]
    lane = lax.broadcasted_iota(jnp.int32, (8, size), 1)
    groups = [a[8 * g : 8 * g + 8] for g in range(size // 8)]
    sub = lax.broadcasted_iota(jnp.int32, (8, size), 0)
    diag = jnp.zeros((1, size), jnp.float32)
    for j in range(size):
        g, s = divmod(j, 8)
        row = groups[g][s : s + 1, :]
        pivot = row[:, j : j + 1]
        inv = lax.rsqrt(pivot)
        inv = inv * (1.5 - 0.5 * pivot * inv * inv)
        at = lane[0:1] == j
        scaled = jnp.where(at, inv, row * inv)
        diag = jnp.where(at, pivot * inv, diag)
        for h in range(g, size // 8):
            f = groups[h][:, j : j + 1] * inv
            new = jnp.where(lane == j, 0.0, groups[h]) - f * scaled
            if h == g:
                new = jnp.where(sub > s, new, jnp.where(sub == s, scaled, groups[h]))
            groups[h] = new
    both = jnp.concatenate(groups, axis=0)
    row = lax.broadcasted_iota(jnp.int32, (size, size), 0)
    col = lax.broadcasted_iota(jnp.int32, (size, size), 1)
    upper = jnp.where(row < col, both, jnp.where(row == col, diag, 0.0))
    return upper.T, jnp.where(row >= col, both, 0.0)


def factor_kernel(me_ref, mine_ref, other_ref, damp_ref, factor_ref, inverse_ref, g_ref, n_ref):
    core = me_ref[0] & 1
    half = mine_ref.shape[0]
    size = factor_ref.shape[0]
    n_ref[pl.ds(pl.multiple_of(core * half, 8), half), :] = mine_ref[...]
    n_ref[pl.ds(pl.multiple_of((1 - core) * half, 8), half), :] = other_ref[...]
    g_ref[...] = n_ref[size : size + 8, :]
    row = lax.broadcasted_iota(jnp.int32, (size, size), 0)
    col = lax.broadcasted_iota(jnp.int32, (size, size), 1)
    n = n_ref[:size, :] + jnp.where(row == col, damp_ref[:, 0:1], 0.0)
    h = size // 2
    l11, i11 = factor_block(n[:h, :h])
    l21 = dot_nt(n[h:, :h], i11, EXACT)
    l22, i22 = factor_block(n[h:, h:] - dot_nt(l21, l21, EXACT))
    i21 = -jnp.dot(i22, jnp.dot(l21, i11, precision=EXACT, preferred_element_type=jnp.float32), precision=EXACT, preferred_element_type=jnp.float32)
    zero = jnp.zeros((h, h), jnp.float32)
    factor_ref[:h, :h] = l11
    factor_ref[:h, h:] = zero
    factor_ref[h:, :h] = l21
    factor_ref[h:, h:] = l22
    inverse_ref[:h, :h] = i11
    inverse_ref[:h, h:] = zero
    inverse_ref[h:, :h] = i21
    inverse_ref[h:, h:] = i22


def last_kernel(bits, n_chunks, n_mirror, me_ref, inverse_ref, g1_ref, mine_ref, other_ref, damp_ref, g2_ref, *refs):
    chunks, mirrors = refs[:n_chunks], refs[n_chunks : n_chunks + n_mirror]
    lower_ref, schur_ref, y_ref, rhs_ref, all_ref = refs[n_chunks + n_mirror :]
    me = me_ref[0]
    own, size = lower_ref.shape
    n = schur_ref.shape[1] // own
    inverse = inverse_ref[...]
    for j in range(n):
        rel = me ^ j
        place = sum(((rel >> bit) & 1) << k for k, bit in enumerate(bits[:-1]))
        far = (rel >> bits[-1]) & 1
        near = mine_ref[place]
        away = other_ref[place]
        all_ref[j * own : (j + 1) * own, :] = jnp.where(far == 1, away, near)
    lower_all = dot_nt(all_ref[...], inverse, EXACT)
    lower = dot_nt(mine_ref[0], inverse, EXACT)
    lower_ref[...] = lower
    whole = jnp.concatenate([c[...] for c in chunks], axis=1)[:, : own * (n_mirror + 2)]
    row = lax.broadcasted_iota(jnp.int32, (own, own), 0)
    col = lax.broadcasted_iota(jnp.int32, (own, own), 1)
    nat = own * STRIDE // (STRIDE - 1)
    target = lax.broadcasted_iota(jnp.int32, (own, nat), 0)
    target = target + 1 + ((target * 9363) >> 16)
    pick = target == lax.broadcasted_iota(jnp.int32, (own, nat), 1)
    damp = jnp.sum(jnp.where(pick, damp_ref[pl.ds(me, 1), :], 0.0), axis=1, keepdims=True)
    first = whole[:, :own] + jnp.where(row == col, damp, 0.0)
    whole = jnp.concatenate([first, whole[:, own:]] + [m[...] for m in reversed(mirrors)], axis=1)
    whole = pltpu.roll(whole, me * own, 1)
    schur_ref[...] = whole - dot_nt(lower, lower_all, EXACT)
    y = dot_nt(g1_ref[...], inverse, EXACT)
    y_ref[...] = y
    rhs_ref[...] = g2_ref[...] - dot_nt(y, lower, EXACT)


def per_device(features, gauge_offset, gauge_count, gauge_resid, damping):
    tiles_here, samples, params = features.shape
    slots = gauge_offset.shape[1]
    axis = "tile"
    n = lax.axis_size(axis)
    bits = n.bit_length() - 1
    panel = params // STRIDE
    trail = params - panel
    own = trail // n
    if 1 << bits != n or n != 16 or own % 16 or params % BLK:
        return per_device_plain(features, gauge_offset, gauge_count, gauge_resid, damping)
    cap = tiles_here * slots // 2
    wide, n_chunks = 256, 4
    count = n // 2 - 1
    half = n // 2
    me = lax.axis_index(axis)
    me1 = me.astype(jnp.int32).reshape(1)
    order = list(range(1, bits))
    orders = [order, order, order, [2, 1] + order[2:]]
    ext = trail + own * half
    padded = panel + 16
    sent, kept, pan_sent, jt, jp, r = call(
        functools.partial(front_kernel, order),
        (me1, gauge_count, gauge_offset, gauge_resid, features.reshape(tiles_here * samples, params)),
        [f32(padded // 2, panel), f32(padded // 2, panel), f32(half, own, panel), bf16(ext, cap), bf16(panel, cap), bf16(16, cap)],
        [pltpu.VMEM((padded, panel), jnp.float32)],
        flops=2 * cap * params * (tiles_here * samples + 2 * panel),
        moved=2 * tiles_here * samples * params,
    )
    n11 = kept + swap(sent, axis, 0)
    pan_got = swap(pan_sent, axis, 0)
    pan_kept, *t_sent = call(
        functools.partial(sent_kernel, orders, order),
        (me1, jt, jp, r),
        [f32(half, own, panel)] + [f32(half, own, wide)] * n_chunks,
        flops=2 * cap * half * own * wide * (n_chunks + 1),
        moved=2 * ext * cap + 4 * half * own * wide * (n_chunks + 1),
    )
    t_got = [swap(x, axis, 0) for x in t_sent]
    t_kept = call(
        functools.partial(kept_kernel, orders),
        (me1, jt, r),
        [f32(half, own, wide)] * n_chunks,
        flops=2 * cap * half * own * wide * n_chunks,
        moved=2 * ext * cap + 4 * half * own * wide * n_chunks,
    )
    for bit in order:
        n11 = n11 + swap(n11, axis, bit)
    n11_other = swap(n11, axis, 0)
    n21 = halve(pan_kept, pan_got, me, order, axis)
    factor, inverse, g1 = call(
        factor_kernel,
        (me1, n11, n11_other, damping.reshape(panel, STRIDE)),
        [f32(panel, panel), f32(panel, panel), f32(8, panel)],
        [pltpu.VMEM((padded, panel), jnp.float32)],
        flops=0,
        moved=100_000_000,
    )
    held = n21[None]
    for bit in reversed(order):
        held = jnp.concatenate([held, swap(held, axis, bit)], axis=0)
    held_other = swap(held, axis, 0)
    chunks = [halve(k, g, me, o, axis) for k, g, o in zip(t_kept, t_got, orders)]
    *blocks, g2 = mirror(chunks, own, count)
    mirrors = [lax.ppermute(b, axis, [(i, (i + k + 1) % n) for i in range(n)]) for k, b in enumerate(blocks)]
    lower, schur, y, rhs = call(
        functools.partial(last_kernel, list(reversed(order)) + [0], n_chunks, count),
        (me1, inverse, g1, held, held_other, damping.reshape(n, params // n), g2, *chunks, *mirrors),
        [f32(own, panel), f32(own, trail), f32(8, panel), f32(8, own)],
        [pltpu.VMEM((trail, panel), jnp.float32)],
        flops=12 * panel * panel * trail,
        moved=8 * trail * panel,
    )
    return (factor, lower, schur, y[0], rhs[0])


def per_device_plain(features, gauge_offset, gauge_count, gauge_resid, damping):
    tiles_here, samples, params = features.shape
    slots = gauge_offset.shape[1]
    panel = params // 8
    trail = params - panel
    rows_here = tiles_here * slots
    slot_ids = lax.broadcasted_iota(jnp.int32, (tiles_here, slots), 1)
    live = slot_ids < gauge_count[:, None]
    sample_ids = lax.broadcasted_iota(jnp.int32, (tiles_here, slots, samples), 2)
    starts = gauge_offset[:, :, None]
    inside = (sample_ids >= starts) & (sample_ids < starts + LWIN) & live[:, :, None]
    window = jnp.where(inside, 1.0 / LWIN, 0.0).astype(jnp.bfloat16)
    jac = jnp.einsum("tgw,twp->tgp", window, features, preferred_element_type=jnp.float32)
    jac = jac.astype(jnp.bfloat16).reshape(rows_here, params)
    resid = jnp.where(live, gauge_resid, jnp.zeros_like(gauge_resid)).reshape(rows_here)
    grad_local = jnp.dot(resid, jac, preferred_element_type=jnp.float32)
    width = lax.axis_size("tile")
    owned = params // width
    owned_trail = owned - owned // 8
    index = lax.axis_index("tile")
    gauges = jac.shape[0]
    jac_split = jac.reshape(gauges, panel, 8)
    jac_panel = jac_split[:, :, 0]
    jac_trail = jac_split[:, :, 1:].reshape(gauges, trail)
    panel_local = lax.dot_general(jac, jac_panel, (((0,), (0,)), ((), ())), preferred_element_type=jnp.float32)
    panel_all, grad = lax.psum((panel_local, grad_local), "tile")
    own_trail = lax.psum_scatter(
        lax.dot_general(jac_trail, jac_trail, (((0,), (0,)), ((), ())), preferred_element_type=jnp.float32),
        "tile",
        scatter_dimension=0,
        tiled=True,
    )
    damp_split = damping.reshape(panel, 8)
    damp_trail = damp_split[:, 1:].reshape(trail)
    trail_ids = index * owned_trail + lax.broadcasted_iota(jnp.int32, (owned_trail, trail), 0)
    column_ids = lax.broadcasted_iota(jnp.int32, (owned_trail, trail), 1)
    own_trail = own_trail + jnp.where(trail_ids == column_ids, damp_trail[None, :], 0.0)
    panel_split = panel_all.reshape(panel, 8, panel)
    n11 = panel_split[:, 0, :] + jnp.diag(damp_split[:, 0])
    n21 = panel_split[:, 1:, :].reshape(trail, panel)
    panel_factor = jnp.linalg.cholesky(n11)
    lower_all = lax.linalg.triangular_solve(panel_factor, n21, left_side=False, lower=True, transpose_a=True)
    lower_own = lax.dynamic_slice_in_dim(lower_all, index * owned_trail, owned_trail, 0)
    schur = own_trail - jnp.dot(lower_own, lower_all.T, precision=lax.Precision.HIGHEST)
    grad_split = grad.reshape(panel, 8)
    first_part = grad_split[:, 0]
    second_part = grad_split[:, 1:].reshape(trail)
    panel_rhs = lax.linalg.triangular_solve(panel_factor, first_part[:, None], left_side=True, lower=True)[:, 0]
    second_own = lax.dynamic_slice_in_dim(second_part, index * owned_trail, owned_trail, 0)
    trail_rhs = second_own - jnp.dot(lower_own, panel_rhs, precision=lax.Precision.HIGHEST)
    return (panel_factor, lower_own, schur, panel_rhs, trail_rhs)


def solution(mesh):
    return jax.shard_map(
        per_device,
        mesh=mesh,
        in_specs=(
            P(("groups", "tile"), None, None),
            P(("groups", "tile"), None),
            P(("groups", "tile")),
            P(("groups", "tile"), None),
            P("groups"),
        ),
        out_specs=(
            P("groups", None),
            P(("groups", "tile"), None),
            P(("groups", "tile"), None),
            P("groups"),
            P(("groups", "tile")),
        ),
        check_vma=False,
    )
```

```python
import functools

import jax
import jax.numpy as jnp
from jax import lax
from jax.experimental import pallas as pl
from jax.experimental.pallas import tpu as pltpu
from jax.sharding import PartitionSpec as P

LWIN = 8
STRIDE = 8
BLK = 256
EXACT = lax.Precision.HIGHEST
VMEM_LIMIT = 56 * 2**20

SMEM_SPEC = pl.BlockSpec(memory_space=pltpu.SMEM)
VMEM_SPEC = pl.BlockSpec(memory_space=pltpu.VMEM)
NT = (((1,), (1,)), ((), ()))


def f32(*shape):
    return jax.ShapeDtypeStruct(shape, jnp.float32)


def bf16(*shape):
    return jax.ShapeDtypeStruct(shape, jnp.bfloat16)


def dot_nt(a, b, precision=None):
    return lax.dot_general(a, b, NT, precision=precision, preferred_element_type=jnp.float32)


def call(kernel, ins, out_shape, scratch=()):
    return pl.pallas_call(
        kernel,
        out_shape=out_shape,
        in_specs=[SMEM_SPEC if x.dtype == jnp.int32 and x.ndim == 1 else VMEM_SPEC for x in ins],
        out_specs=jax.tree.map(lambda _: VMEM_SPEC, out_shape),
        scratch_shapes=list(scratch),
        compiler_params=pltpu.CompilerParams(vmem_limit_bytes=VMEM_LIMIT),
        cost_estimate=pl.CostEstimate(flops=1, bytes_accessed=1, transcendentals=0),
    )(*ins)


def owner_of(m, order):
    last = len(order) - 1
    return sum(((m >> (last - k)) & 1) << bit for k, bit in enumerate(order))


def front_kernel(order, me_ref, count_ref, offset_ref, resid_ref, feat_ref, sent_ref, kept_ref, jt_ref, r_ref, jp_ref, n21_ref):
    tiles, slots = offset_ref.shape
    depth, params = feat_ref.shape
    samples = depth // tiles
    cap = jp_ref.shape[1]
    panel = jp_ref.shape[0]
    trail = params - panel
    core = me_ref[0] & 1
    lane = lax.broadcasted_iota(jnp.int32, (8, cap), 1)
    start = jnp.full((8, cap), -depth, jnp.int32)
    resid = jnp.zeros((8, cap), jnp.float32)
    before = jnp.int32(0)
    for t in range(tiles):
        count = count_ref[t]
        live = (lane >= before) & (lane < before + count)
        offs = jnp.concatenate([offset_ref[t : t + 1, :], jnp.zeros((1, cap - slots), jnp.int32)], axis=1)
        offs = pltpu.roll(jnp.broadcast_to(offs, (8, cap)), before, 1)
        res = jnp.concatenate([resid_ref[t : t + 1, :].astype(jnp.float32), jnp.zeros((1, cap - slots), jnp.float32)], axis=1)
        res = pltpu.roll(jnp.broadcast_to(res, (8, cap)), before, 1)
        start = jnp.where(live, offs + t * samples, start)
        resid = jnp.where(live, res, resid)
        before = before + count
    first = lax.broadcasted_iota(jnp.int32, (8, cap), 0) == 0
    resid = jnp.where(first, resid, 0.0).astype(jnp.bfloat16)
    r_ref[...] = jnp.concatenate([resid, jnp.zeros((8, cap), jnp.bfloat16)], axis=0)
    after = lax.broadcasted_iota(jnp.int32, (depth, cap), 0) - start[0:1, :]
    window = jnp.where((after >= 0) & (after < LWIN), 1.0 / LWIN, 0.0).astype(jnp.bfloat16)
    pan_b = BLK // STRIDE
    row = lax.broadcasted_iota(jnp.int32, (BLK, BLK), 0)
    col = lax.broadcasted_iota(jnp.int32, (BLK, BLK), 1)
    rest = row - pan_b
    source = jnp.where(row < pan_b, row * STRIDE, rest + 1 + ((rest * 9363) >> 16))
    pick = jnp.where(source == col, 1.0, 0.0).astype(jnp.bfloat16)
    trail_b = BLK - pan_b
    for b in range(params // BLK):
        turned = dot_nt(pick, feat_ref[:, b * BLK : (b + 1) * BLK]).astype(jnp.bfloat16)
        jac = jnp.dot(turned, window, preferred_element_type=jnp.float32).astype(jnp.bfloat16)
        jp_ref[b * pan_b : (b + 1) * pan_b, :] = jac[:pan_b]
        jt_ref[b * trail_b : (b + 1) * trail_b, :] = jac[pan_b:]
        if trail + (b + 1) * trail_b <= jt_ref.shape[0]:
            jt_ref[trail + b * trail_b : trail + (b + 1) * trail_b, :] = jac[pan_b:]
    jp = jp_ref[...]
    n21_ref[...] = dot_nt(jt_ref[:trail, :], jp)
    own, count = sent_ref.shape[1], sent_ref.shape[0] - 1
    for m in range(count):
        base = owner_of(m, order) * own
        sent_ref[m] = n21_ref[pl.ds(pl.multiple_of(base + (1 - core) * own, 16), own), :]
        kept_ref[m] = n21_ref[pl.ds(pl.multiple_of(base + core * own, 16), own), :]
    half, rows = panel // 2, panel // 4
    n21_ref[:panel, :] = dot_nt(jp, jp)
    grad = dot_nt(r_ref[...], jp)
    for ref, which in ((sent_ref, 1 - core), (kept_ref, core)):
        for side in range(2):
            lanes = slice(side * half, (side + 1) * half)
            at = pl.multiple_of(which * half + side * rows, 16)
            first = n21_ref[pl.ds(at, rows), :]
            ref[count, :rows, lanes] = jnp.where(which == 1, first[:, half:], first[:, :half])
            at = pl.multiple_of(half + which * rows + side * (rows // 2), 16)
            ref[count, rows : rows + rows // 2, lanes] = n21_ref[pl.ds(at, rows // 2), :half]
        ref[count, rows + rows // 2 :, :] = grad[: own - rows - rows // 2]


def trail_kernel(me_ref, jt_ref, r_ref, sent1_ref, sent2_ref, kept1_ref, kept2_ref, pair_ref):
    base = pl.program_id(0) * 2 * sent1_ref.shape[1]
    core = me_ref[0] & 1
    own, wide = sent1_ref.shape[1:]
    end = wide + sent2_ref.shape[2]
    real = end - r_ref.shape[0]
    rows = jt_ref[pl.ds(pl.multiple_of(base, 16), 2 * own), :]
    others = jt_ref[pl.ds(pl.multiple_of(base, 16), real + own), :]
    both = dot_nt(rows, others)
    last = dot_nt(rows, r_ref[...])
    pair_ref[0, :, :real] = both[:own, :real]
    pair_ref[0, :, real:] = last[:own]
    pair_ref[1, :, :real] = both[own:, own:]
    pair_ref[1, :, real:] = last[own:]
    for first, second, which in ((sent1_ref, sent2_ref, 1 - core), (kept1_ref, kept2_ref, core)):
        first[0] = pair_ref[which, :, :wide]
        second[0] = pair_ref[which, :, wide:]


def place_of(m, order):
    return sum(((m >> (bit - 1)) & 1) << (len(order) - 1 - k) for k, bit in enumerate(order))


def trailing(me1, jt, r, orders, half, own, widths):
    def spec(order, wide):
        return pl.BlockSpec((1, own, wide), lambda m: (place_of(m, order), 0, 0))

    return pl.pallas_call(
        trail_kernel,
        grid=(half,),
        out_shape=[f32(half, own, wide) for wide in widths] * 2,
        in_specs=[SMEM_SPEC, pl.BlockSpec(jt.shape, lambda m: (0, 0)), pl.BlockSpec(r.shape, lambda m: (0, 0))],
        out_specs=[spec(order, wide) for order, wide in zip(orders, widths)] * 2,
        scratch_shapes=[pltpu.VMEM((2, own, sum(widths)), jnp.float32)],
        compiler_params=pltpu.CompilerParams(vmem_limit_bytes=VMEM_LIMIT),
        cost_estimate=pl.CostEstimate(flops=1, bytes_accessed=1, transcendentals=0),
    )(me1, jt, r)


def swap(x, axis, bit):
    n = lax.axis_size(axis)
    return lax.ppermute(x, axis, [(i, i ^ (1 << bit)) for i in range(n)])


def panel_fold_kernel(bit, me_ref, kept_ref, got_ref, sent_out, kept_out):
    mine = (me_ref[0] >> bit) & 1
    size = kept_out.shape[0] - 1
    for k in range(size):
        sent_out[k] = kept_ref[(1 - mine) * size + k] + got_ref[(1 - mine) * size + k]
        kept_out[k] = kept_ref[mine * size + k] + got_ref[mine * size + k]
    total = kept_ref[2 * size] + got_ref[2 * size]
    sent_out[size] = total
    kept_out[size] = total


def fold(kept, got, me, bit):
    mine = (me >> bit) & 1
    size = kept.shape[0] // 2
    kept = kept.reshape((2, size) + kept.shape[1:])
    got = got.reshape(kept.shape)

    def part(which):
        return lax.dynamic_index_in_dim(kept, which, 0, False) + lax.dynamic_index_in_dim(got, which, 0, False)

    return part(1 - mine), part(mine)


def mirror(sums, own, ks, row):
    flat = [x for pair in sums for x in pair]
    widths = [pair[0].shape[-1] for pair in sums]
    new = [len(pair) == 2 for pair in sums]
    total = sum(widths)

    def kernel(*refs):
        ins, outs = list(refs[: len(flat)]), list(refs[len(flat) :])
        turned_ref = outs.pop()
        at = 0
        for wide, pair in zip(widths, new):
            x = ins.pop(0)
            x = x[0] + ins.pop(0)[0] if pair else x[...]
            if pair:
                outs.pop(0)[...] = x
            turned_ref[at : at + wide, :] = x.T
            at += wide
        for k in ks:
            outs.pop(0)[...] = turned_ref[k * own : (k + 1) * own, :]
        if row:
            outs.pop(0)[...] = turned_ref[row : row + 8, :]

    shapes = [f32(own, w) for w, pair in zip(widths, new) if pair] + [f32(own, own)] * len(ks) + [f32(8, own)] * bool(row)
    out = list(call(kernel, flat, shapes, [pltpu.VMEM((total, own), jnp.float32)]))
    return out[: sum(new)], out[sum(new) : sum(new) + len(ks)], out[-1]


def factor_block(a):
    size = a.shape[0]
    shape = (8, size)
    lane = lax.broadcasted_iota(jnp.int32, shape, 1)
    sub = lax.broadcasted_iota(jnp.int32, shape, 0)
    groups = [a[at : at + 8] for at in range(0, size, 8)]

    def column(x, j):
        return jnp.broadcast_to(x[:, j : j + 1], shape)

    def row(x, s):
        return jnp.broadcast_to(x[s : s + 1, :], shape)

    uppers, lowers = [], []
    for g, x in enumerate(groups):
        first = 8 * g
        inside = (lane >= first) & (lane < first + 8)
        columns = [column(x, first + k) for k in range(8)]
        pivots = jnp.zeros(shape, jnp.float32)
        inverses, rows, cross = [], [], {}
        for k in range(8):
            pivot = row(columns[k], k)
            inverse = pltpu.reciprocal(pivot, approx=True)
            inverse = inverse * (2.0 - pivot * inverse)
            scaled = columns[k] * inverse
            for m in range(k + 1, 8):
                cross[k, m] = row(columns[m], k)
                columns[m] = columns[m] - scaled * cross[k, m]
            at = lane == first + k
            this = jnp.where(at, 1.0, row(x, k))
            x = jnp.where(at & (sub >= k), jnp.where(sub == k, 1.0, 0.0), x) - jnp.where(sub > k, scaled, 0.0) * this
            pivots = jnp.where(sub == k, pivot, pivots)
            inverses.append(inverse)
            rows.append(jnp.where(inside & (lane > first + k), 0.0, this))
        for h in range(g + 1, len(groups)):
            below = groups[h]
            columns = [column(below, first + k) for k in range(8)]
            below = jnp.where(inside, 0.0, below)
            for k in range(8):
                scaled = columns[k] * inverses[k]
                for m in range(k + 1, 8):
                    columns[m] = columns[m] - scaled * cross[k, m]
                below = below - scaled * rows[k]
            groups[h] = below
        root = lax.rsqrt(pivots)
        root = root * (1.5 - 0.5 * pivots * root * root)
        scaled = x * root
        off = lane - first - sub
        uppers.append(jnp.where(off > 0, scaled, jnp.where(off == 0, pivots * root, 0.0)))
        lowers.append(jnp.where(off <= 0, scaled, 0.0))
    return jnp.concatenate(uppers, axis=0).T, jnp.concatenate(lowers, axis=0)


def factor_first_kernel(me_ref, mine_ref, other_ref, damp_ref, g_ref, l11_ref, i11_ref, l21_ref, rest_ref):
    core = me_ref[0] & 1
    half = l11_ref.shape[0]
    rows = half // 2
    mine, other = mine_ref[0], other_ref[0]
    low, high = jnp.where(core == 0, mine, other), jnp.where(core == 0, other, mine)

    def opened(x):
        return jnp.concatenate([x[:, :half], x[:, half:]], axis=0)

    row = lax.broadcasted_iota(jnp.int32, (half, half), 0)
    col = lax.broadcasted_iota(jnp.int32, (half, half), 1)
    n11 = opened(low[:rows]) + jnp.where(row == col, damp_ref[:half, 0:1], 0.0)
    n22 = opened(high[:rows]) + jnp.where(row == col, damp_ref[half:, 0:1], 0.0)
    n21 = jnp.concatenate([opened(x[rows : rows + rows // 2]) for x in (low, high)], axis=0)
    g_ref[...] = mine[rows + rows // 2 : rows + rows // 2 + 8]
    l11, i11 = factor_block(n11)
    l21 = dot_nt(n21, i11, EXACT)
    l11_ref[...] = l11
    i11_ref[...] = i11
    l21_ref[...] = l21
    rest_ref[...] = n22 - dot_nt(l21, l21, EXACT)


def factor_second_kernel(l11_ref, i11_ref, l21_ref, rest_ref, factor_ref, inverse_ref):
    half = l11_ref.shape[0]
    l22, i22 = factor_block(rest_ref[...])
    before = jnp.dot(l21_ref[...], i11_ref[...], precision=EXACT, preferred_element_type=jnp.float32)
    zero = jnp.zeros((half, half), jnp.float32)
    factor_ref[:half, :half] = l11_ref[...]
    factor_ref[:half, half:] = zero
    factor_ref[half:, :half] = l21_ref[...]
    factor_ref[half:, half:] = l22
    inverse_ref[:half, :half] = i11_ref[...]
    inverse_ref[:half, half:] = zero
    inverse_ref[half:, :half] = -jnp.dot(i22, before, precision=EXACT, preferred_element_type=jnp.float32)
    inverse_ref[half:, half:] = i22


def lower_kernel(inverse_ref, g1_ref, held_ref, lower_ref, out_ref, y_ref, flat_ref):
    inverse = inverse_ref[...]
    count, own, size = held_ref.shape
    lower = dot_nt(held_ref[...].reshape(count * own, size), inverse, EXACT).reshape(count, own, size)
    lower_ref[...] = lower
    out_ref[...] = lower[0]
    y = dot_nt(g1_ref[...], inverse, EXACT)
    y_ref[...] = y
    flat_ref[...] = y[0]


def product_kernel(bits, me_ref, mine_ref, other_ref, product_ref, all_ref):
    me = me_ref[0]
    own = product_ref.shape[0]
    for k in range(mine_ref.shape[0]):
        owner = me ^ sum(((k >> i) & 1) << bit for i, bit in enumerate(bits))
        all_ref[pl.ds(pl.multiple_of(owner * own, 16), own), :] = mine_ref[k]
        all_ref[pl.ds(pl.multiple_of((owner ^ 1) * own, 16), own), :] = other_ref[k]
    product_ref[...] = dot_nt(mine_ref[0], all_ref[...], EXACT)


def last_kernel(n_chunks, me_ref, damp_ref, product_ref, g2_ref, y_ref, lower_ref, *refs):
    chunks, mirrors, (schur_ref, rhs_ref) = refs[:n_chunks], refs[n_chunks:-2], refs[-2:]
    rhs_ref[...] = (g2_ref[...] - dot_nt(y_ref[...], lower_ref[...], EXACT))[0]
    me = me_ref[0]
    own = schur_ref.shape[0]
    whole = jnp.concatenate([c[...] for c in chunks], axis=1)[:, : own * (len(mirrors) + 2)]
    row = lax.broadcasted_iota(jnp.int32, (own, own), 0)
    col = lax.broadcasted_iota(jnp.int32, (own, own), 1)
    nat = own * STRIDE // (STRIDE - 1)
    target = lax.broadcasted_iota(jnp.int32, (own, nat), 0)
    target = target + 1 + ((target * 9363) >> 16)
    pick = target == lax.broadcasted_iota(jnp.int32, (own, nat), 1)
    damp = jnp.sum(jnp.where(pick, damp_ref[pl.ds(me, 1), :], 0.0), axis=1, keepdims=True)
    first = whole[:, :own] + jnp.where(row == col, damp, 0.0)
    whole = jnp.concatenate([first, whole[:, own:]] + [m[...] for m in reversed(mirrors)], axis=1)
    schur_ref[...] = pltpu.roll(whole, me * own, 1) - product_ref[...]


def per_device(features, gauge_offset, gauge_count, gauge_resid, damping):
    tiles_here, samples, params = features.shape
    slots = gauge_offset.shape[1]
    axis = "tile"
    n = lax.axis_size(axis)
    panel = params // STRIDE
    trail = params - panel
    own = trail // n
    if n != 16 or own != 112 or params % BLK:
        return per_device_plain(features, gauge_offset, gauge_count, gauge_resid, damping)
    cap = tiles_here * slots // 2
    count = n // 2 - 1
    half = n // 2
    widths = (640, 384)
    me = lax.axis_index(axis)
    me1 = me.astype(jnp.int32).reshape(1)
    order = [1, 2, 3]
    orders = [order, order]
    ext = trail + own * half
    last = [()]

    def then(*xs):
        xs, last[0] = lax.optimization_barrier((xs, last[0]))
        return xs

    def did(x):
        last[0] = x
        return x

    sent, p, jt, r = did(
        call(
            functools.partial(front_kernel, order),
            (me1, gauge_count, gauge_offset, gauge_resid, features.reshape(tiles_here * samples, params)),
            [f32(half + 1, own, panel)] * 2 + [bf16(ext, cap), bf16(16, cap)],
            [pltpu.VMEM((panel, cap), jnp.bfloat16), pltpu.VMEM((trail, panel), jnp.float32)],
        )
    )
    p_got = swap(sent, axis, 0)
    t, t_got = [None, None], [None, None]

    def panel_fold(p, got, bit):
        shape = f32(p.shape[0] // 2 + 1, *p.shape[1:])
        sent, p = did(call(functools.partial(panel_fold_kernel, bit), then(me1, p, got), [shape] * 2))
        return p, swap(sent, axis, bit)

    def trail_fold(q, step):
        bit = orders[q][step]
        sent, t[q] = did(fold(*then(t[q], t_got[q]), me, bit))
        t_sent[q] = sent

    def trail_send(q, step):
        t_got[q] = swap(t_sent[q], axis, orders[q][step])

    def trail_step(q, step):
        trail_fold(q, step)
        trail_send(q, step)

    def joined(held, got):
        return did(jnp.concatenate(then(held, got), axis=0))

    t_sent = [None, None]
    p, p_got = panel_fold(p, p_got, order[0])
    *t_sent, t[0], t[1] = did(trailing(*then(me1, jt, r), orders, half, own, widths))
    t_sent, p_got = lax.optimization_barrier((t_sent, p_got))
    t_got = [swap(x, axis, 0) for x in t_sent]
    p, p_got = panel_fold(p, p_got, order[1])
    trail_step(0, 0)
    p, p_got = panel_fold(p, p_got, order[2])
    trail_step(1, 0)
    damp_panel, damp_trail = then(damping)[0].reshape(panel, STRIDE), damping.reshape(n, params // n)
    damp_panel = did(damp_panel)
    p, p_got = then(p, p_got)
    p = did(p + p_got)
    held, n11 = p[:1], p[1:]
    n11_got = swap(n11, axis, 0)
    got = swap(held, axis, order[2])
    g1, *state = did(
        call(factor_first_kernel, then(me1, n11, n11_got, damp_panel), [f32(8, panel)] + [f32(panel // 2, panel // 2)] * 4)
    )
    held = joined(held, got)
    got = swap(held, axis, order[1])
    trail_step(0, 1)
    factor, inverse = did(call(factor_second_kernel, then(*state), [f32(panel, panel)] * 2))
    held = joined(held, got)
    got = swap(held, axis, order[0])
    trail_step(1, 1)
    trail_step(0, 2)
    held = joined(held, got)
    mine, lower, y, y0 = did(
        call(lower_kernel, then(inverse, g1, held), [f32(half, own, panel), f32(own, panel), f32(8, panel), f32(panel)])
    )
    trail_step(1, 2)
    other = swap(lax.optimization_barrier((mine, t[1]))[0], axis, 0)
    ks = [range(1, widths[0] // own), range(widths[0] // own, count + 1)]
    (c0,), blocks, _ = did(mirror([then(t[0], t_got[0])], own, ks[0], 0))

    def mirrored(blocks, ks):
        return [lax.ppermute(b, axis, [(i, (i + k) % n) for i in range(n)]) for k, b in zip(ks, blocks)]

    mirrors = mirrored(blocks, ks[0])
    product = did(
        call(
            functools.partial(product_kernel, list(reversed(order))),
            then(me1, mine, other),
            f32(own, trail),
            [pltpu.VMEM((trail, panel), jnp.float32)],
        )
    )
    (c1,), blocks, g2 = did(mirror([(c0,), then(t[1], t_got[1])], own, ks[1], (count + 2) * own))
    mirrors += mirrored(blocks, ks[1])
    chunks = [c0, c1]
    schur, rhs0 = call(
        functools.partial(last_kernel, 2),
        then(me1, damp_trail, product, g2, y, lower, *chunks, *mirrors),
        [f32(own, trail), f32(own)],
    )
    return (factor, lower, schur, y0, rhs0)


def per_device_plain(features, gauge_offset, gauge_count, gauge_resid, damping):
    tiles_here, samples, params = features.shape
    slots = gauge_offset.shape[1]
    panel = params // 8
    trail = params - panel
    rows_here = tiles_here * slots
    slot_ids = lax.broadcasted_iota(jnp.int32, (tiles_here, slots), 1)
    live = slot_ids < gauge_count[:, None]
    sample_ids = lax.broadcasted_iota(jnp.int32, (tiles_here, slots, samples), 2)
    starts = gauge_offset[:, :, None]
    inside = (sample_ids >= starts) & (sample_ids < starts + LWIN) & live[:, :, None]
    window = jnp.where(inside, 1.0 / LWIN, 0.0).astype(jnp.bfloat16)
    jac = jnp.einsum("tgw,twp->tgp", window, features, preferred_element_type=jnp.float32)
    jac = jac.astype(jnp.bfloat16).reshape(rows_here, params)
    resid = jnp.where(live, gauge_resid, jnp.zeros_like(gauge_resid)).reshape(rows_here)
    grad_local = jnp.dot(resid, jac, preferred_element_type=jnp.float32)
    width = lax.axis_size("tile")
    owned = params // width
    owned_trail = owned - owned // 8
    index = lax.axis_index("tile")
    gauges = jac.shape[0]
    jac_split = jac.reshape(gauges, panel, 8)
    jac_panel = jac_split[:, :, 0]
    jac_trail = jac_split[:, :, 1:].reshape(gauges, trail)
    panel_local = lax.dot_general(jac, jac_panel, (((0,), (0,)), ((), ())), preferred_element_type=jnp.float32)
    panel_all, grad = lax.psum((panel_local, grad_local), "tile")
    own_trail = lax.psum_scatter(
        lax.dot_general(jac_trail, jac_trail, (((0,), (0,)), ((), ())), preferred_element_type=jnp.float32),
        "tile",
        scatter_dimension=0,
        tiled=True,
    )
    damp_split = damping.reshape(panel, 8)
    damp_trail = damp_split[:, 1:].reshape(trail)
    trail_ids = index * owned_trail + lax.broadcasted_iota(jnp.int32, (owned_trail, trail), 0)
    column_ids = lax.broadcasted_iota(jnp.int32, (owned_trail, trail), 1)
    own_trail = own_trail + jnp.where(trail_ids == column_ids, damp_trail[None, :], 0.0)
    panel_split = panel_all.reshape(panel, 8, panel)
    n11 = panel_split[:, 0, :] + jnp.diag(damp_split[:, 0])
    n21 = panel_split[:, 1:, :].reshape(trail, panel)
    panel_factor = jnp.linalg.cholesky(n11)
    lower_all = lax.linalg.triangular_solve(panel_factor, n21, left_side=False, lower=True, transpose_a=True)
    lower_own = lax.dynamic_slice_in_dim(lower_all, index * owned_trail, owned_trail, 0)
    schur = own_trail - jnp.dot(lower_own, lower_all.T, precision=lax.Precision.HIGHEST)
    grad_split = grad.reshape(panel, 8)
    first_part = grad_split[:, 0]
    second_part = grad_split[:, 1:].reshape(trail)
    panel_rhs = lax.linalg.triangular_solve(panel_factor, first_part[:, None], left_side=True, lower=True)[:, 0]
    second_own = lax.dynamic_slice_in_dim(second_part, index * owned_trail, owned_trail, 0)
    trail_rhs = second_own - jnp.dot(lower_own, panel_rhs, precision=lax.Precision.HIGHEST)
    return (panel_factor, lower_own, schur, panel_rhs, trail_rhs)


def solution(mesh):
    return jax.shard_map(
        per_device,
        mesh=mesh,
        in_specs=(
            P(("groups", "tile"), None, None),
            P(("groups", "tile"), None),
            P(("groups", "tile")),
            P(("groups", "tile"), None),
            P("groups"),
        ),
        out_specs=(
            P("groups", None),
            P(("groups", "tile"), None),
            P(("groups", "tile"), None),
            P("groups"),
            P(("groups", "tile")),
        ),
        check_vma=False,
    )
```

```python
import functools

import jax
import jax.numpy as jnp
from jax import lax
from jax.experimental import pallas as pl
from jax.experimental.pallas import tpu as pltpu
from jax.sharding import PartitionSpec as P

LWIN = 8
STRIDE = 8
BLK = 256
EXACT = lax.Precision.HIGHEST
VMEM_LIMIT = 56 * 2**20

SMEM_SPEC = pl.BlockSpec(memory_space=pltpu.SMEM)
VMEM_SPEC = pl.BlockSpec(memory_space=pltpu.VMEM)
NT = (((1,), (1,)), ((), ()))


def f32(*shape):
    return jax.ShapeDtypeStruct(shape, jnp.float32)


def bf16(*shape):
    return jax.ShapeDtypeStruct(shape, jnp.bfloat16)


def dot_nt(a, b, precision=None):
    return lax.dot_general(a, b, NT, precision=precision, preferred_element_type=jnp.float32)


def call(kernel, ins, out_shape, scratch=()):
    return pl.pallas_call(
        kernel,
        out_shape=out_shape,
        in_specs=[SMEM_SPEC if x.dtype == jnp.int32 and x.ndim == 1 else VMEM_SPEC for x in ins],
        out_specs=jax.tree.map(lambda _: VMEM_SPEC, out_shape),
        scratch_shapes=list(scratch),
        compiler_params=pltpu.CompilerParams(vmem_limit_bytes=VMEM_LIMIT),
        cost_estimate=pl.CostEstimate(flops=1, bytes_accessed=1, transcendentals=0),
    )(*ins)


def owner_of(m, order):
    last = len(order) - 1
    return sum(((m >> (last - k)) & 1) << bit for k, bit in enumerate(order))


def front_kernel(
    order, me_ref, count_ref, offset_ref, resid_ref, feat_hbm, sent_hbm, kept_hbm, jt_hbm, r_ref,
    feat_ref, jp_ref, jt_ref, n21_ref, n11_ref, pack_ref, feat_sems, jt_sems, out_sems,
):
    depth, params = feat_ref.shape
    blocks = params // BLK
    core = me_ref[0] & 1
    pan_b = BLK // STRIDE
    trail_b = BLK - pan_b
    feat_copies = [
        pltpu.make_async_copy(feat_hbm.at[:, b * BLK : (b + 1) * BLK], feat_ref.at[:, b * BLK : (b + 1) * BLK], feat_sems.at[b])
        for b in range(blocks)
    ]
    for copy in feat_copies:
        copy.start()
    window, pick = window_part(count_ref, offset_ref, resid_ref, depth, jp_ref.shape[1], r_ref)
    copies = []
    for b in range(blocks):
        feat_copies[b].wait()
        turned = dot_nt(pick, feat_ref[:, b * BLK : (b + 1) * BLK]).astype(jnp.bfloat16)
        jac = jnp.dot(turned, window, preferred_element_type=jnp.float32).astype(jnp.bfloat16)
        jp_ref[b * pan_b : (b + 1) * pan_b, :] = jac[:pan_b]
        rows = slice(b * trail_b, (b + 1) * trail_b)
        jt_ref[rows, :] = jac[pan_b:]
        copies.append(pltpu.make_async_copy(jt_ref.at[rows], jt_hbm.at[rows], jt_sems.at[b]))
        copies[-1].start()
    jp = jp_ref[...]
    own, count = sent_hbm.shape[1], sent_hbm.shape[0] - 1
    ways = ((sent_hbm, 1 - core), (kept_hbm, core))
    panel = jp.shape[0]
    half, part = panel // 2, panel // 4
    n11_ref[...] = dot_nt(jp, jp)
    grad = dot_nt(r_ref[...], jp)
    for k, (out, which) in enumerate(ways):
        for side in range(2):
            lanes = slice(side * half, (side + 1) * half)
            at = pl.multiple_of(which * half + side * part, 16)
            first = n11_ref[pl.ds(at, part), :]
            pack_ref[k, :part, lanes] = jnp.where(which == 1, first[:, half:], first[:, :half])
            at = pl.multiple_of(half + which * part + side * (part // 2), 16)
            pack_ref[k, part : part + part // 2, lanes] = n11_ref[pl.ds(at, part // 2), :half]
        pack_ref[k, part + part // 2 :, :] = grad[: own - part - part // 2]
        copies.append(pltpu.make_async_copy(pack_ref.at[k], out.at[count], out_sems.at[k, count]))
        copies[-1].start()
    for m in range(count):
        rows = slice(m * 2 * own, (m + 1) * 2 * own)
        n21_ref[rows, :] = dot_nt(jt_ref[rows, :], jp)
        for k, (out, which) in enumerate(ways):
            source = n21_ref.at[pl.ds(pl.multiple_of(m * 2 * own + which * own, 16), own), :]
            copies.append(pltpu.make_async_copy(source, out.at[place_of(m, order)], out_sems.at[k, m]))
            copies[-1].start()
    for copy in copies:
        copy.wait()


def window_part(count_ref, offset_ref, resid_ref, depth, cap, r_ref):
    tiles, slots = offset_ref.shape
    samples = depth // tiles
    lane = lax.broadcasted_iota(jnp.int32, (8, cap), 1)
    start = jnp.full((8, cap), -depth, jnp.int32)
    resid = jnp.zeros((8, cap), jnp.float32)
    before = jnp.int32(0)
    for t in range(tiles):
        count = count_ref[t]
        live = (lane >= before) & (lane < before + count)
        offs = jnp.concatenate([offset_ref[t : t + 1, :], jnp.zeros((1, cap - slots), jnp.int32)], axis=1)
        offs = pltpu.roll(jnp.broadcast_to(offs, (8, cap)), before, 1)
        res = jnp.concatenate([resid_ref[t : t + 1, :].astype(jnp.float32), jnp.zeros((1, cap - slots), jnp.float32)], axis=1)
        res = pltpu.roll(jnp.broadcast_to(res, (8, cap)), before, 1)
        start = jnp.where(live, offs + t * samples, start)
        resid = jnp.where(live, res, resid)
        before = before + count
    first = lax.broadcasted_iota(jnp.int32, (8, cap), 0) == 0
    resid = jnp.where(first, resid, 0.0).astype(jnp.bfloat16)
    r_ref[...] = jnp.concatenate([resid, jnp.zeros((8, cap), jnp.bfloat16)], axis=0)
    after = lax.broadcasted_iota(jnp.int32, (depth, cap), 0) - start[0:1, :]
    window = jnp.where((after >= 0) & (after < LWIN), 1.0 / LWIN, 0.0).astype(jnp.bfloat16)
    pan_b = BLK // STRIDE
    row = lax.broadcasted_iota(jnp.int32, (BLK, BLK), 0)
    col = lax.broadcasted_iota(jnp.int32, (BLK, BLK), 1)
    rest = row - pan_b
    source = jnp.where(row < pan_b, row * STRIDE, rest + 1 + ((rest * 9363) >> 16))
    return window, jnp.where(source == col, 1.0, 0.0).astype(jnp.bfloat16)


def trail_kernel(me_ref, jt_hbm, r_ref, *refs):
    outs, (pair_ref, jt_ref, sems) = refs[:-3], refs[-3:]
    sent, kept = outs[: len(outs) // 2], outs[len(outs) // 2 :]
    m = pl.program_id(0)
    core = me_ref[0] & 1
    own = sent[0].shape[1]
    base = m * 2 * own
    pairs = jt_hbm.shape[0] // (2 * own)
    ahead = jt_ref.shape[0] // (2 * own) - pairs

    def brought(k):
        source = jt_hbm.at[pl.ds(pl.multiple_of(lax.rem(k, pairs) * 2 * own, 16), 2 * own), :]
        return pltpu.make_async_copy(source, jt_ref.at[pl.ds(pl.multiple_of(k * 2 * own, 16), 2 * own), :], sems.at[k])

    @pl.when(m == 0)
    def _():
        for k in range(pairs + ahead):
            brought(jnp.int32(k)).start()
        for k in range(ahead):
            brought(jnp.int32(k)).wait()

    brought(m + ahead).wait()
    real = pair_ref.shape[2] - r_ref.shape[0]
    rows = jt_ref[pl.ds(pl.multiple_of(base, 16), 2 * own), :]
    others = jt_ref[pl.ds(pl.multiple_of(base, 16), real + own), :]
    both = dot_nt(rows, others)
    last = dot_nt(rows, r_ref[...])
    pair_ref[0, :, :real] = both[:own, :real]
    pair_ref[0, :, real:] = last[:own]
    pair_ref[1, :, :real] = both[own:, own:]
    pair_ref[1, :, real:] = last[own:]
    for group, which in ((sent, 1 - core), (kept, core)):
        at = 0
        for ref in group:
            ref[0] = pair_ref[which, :, at : at + ref.shape[2]]
            at += ref.shape[2]


def place_of(m, order):
    return sum(((m >> (bit - 1)) & 1) << (len(order) - 1 - k) for k, bit in enumerate(order))


def trailing(me1, jt, r, orders, half, own, widths):
    def spec(order, wide):
        return pl.BlockSpec((1, own, wide), lambda m: (place_of(m, order), 0, 0))

    pairs = half + half // 2
    return pl.pallas_call(
        trail_kernel,
        grid=(half,),
        out_shape=[f32(half, own, wide) for wide in widths] * 2,
        in_specs=[SMEM_SPEC, pl.BlockSpec(memory_space=pl.ANY), pl.BlockSpec(r.shape, lambda m: (0, 0))],
        out_specs=[spec(order, wide) for order, wide in zip(orders, widths)] * 2,
        scratch_shapes=[
            pltpu.VMEM((2, own, sum(widths)), jnp.float32),
            pltpu.VMEM((2 * own * pairs, jt.shape[1]), jnp.bfloat16),
            pltpu.SemaphoreType.DMA((pairs,)),
        ],
        compiler_params=pltpu.CompilerParams(vmem_limit_bytes=VMEM_LIMIT),
        cost_estimate=pl.CostEstimate(flops=1, bytes_accessed=1, transcendentals=0),
    )(me1, jt, r)


def front(order, me1, gauge_count, gauge_offset, gauge_resid, feats, half, own):
    depth, params = feats.shape
    cap = gauge_offset.size // 2
    panel = params // STRIDE
    trail = params - panel
    hbm = pl.BlockSpec(memory_space=pl.ANY)
    return pl.pallas_call(
        functools.partial(front_kernel, order),
        out_shape=[f32(half + 1, own, panel)] * 2 + [bf16(trail, cap), bf16(16, cap)],
        in_specs=[SMEM_SPEC, SMEM_SPEC, VMEM_SPEC, VMEM_SPEC, hbm],
        out_specs=[hbm, hbm, hbm, VMEM_SPEC],
        scratch_shapes=[
            pltpu.VMEM((depth, params), jnp.bfloat16),
            pltpu.VMEM((panel, cap), jnp.bfloat16),
            pltpu.VMEM((trail, cap), jnp.bfloat16),
            pltpu.VMEM((trail, panel), jnp.float32),
            pltpu.VMEM((panel, panel), jnp.float32),
            pltpu.VMEM((2, own, panel), jnp.float32),
            pltpu.SemaphoreType.DMA((params // BLK,)),
            pltpu.SemaphoreType.DMA((params // BLK,)),
            pltpu.SemaphoreType.DMA((2, half + 1)),
        ],
        compiler_params=pltpu.CompilerParams(vmem_limit_bytes=VMEM_LIMIT),
        cost_estimate=pl.CostEstimate(flops=1, bytes_accessed=1, transcendentals=0),
    )(me1, gauge_count, gauge_offset, gauge_resid, feats)


def swap(x, axis, bit):
    n = lax.axis_size(axis)
    return lax.ppermute(x, axis, [(i, i ^ (1 << bit)) for i in range(n)])


def panel_fold_kernel(bit, me_ref, kept_ref, got_ref, sent_out, kept_out):
    mine = (me_ref[0] >> bit) & 1
    size = kept_out.shape[0] - 1
    for k in range(size):
        sent_out[k] = kept_ref[(1 - mine) * size + k] + got_ref[(1 - mine) * size + k]
        kept_out[k] = kept_ref[mine * size + k] + got_ref[mine * size + k]
    total = kept_ref[2 * size] + got_ref[2 * size]
    sent_out[size] = total
    kept_out[size] = total


def fold(kept, got, me, bit):
    mine = (me >> bit) & 1
    size = kept.shape[0] // 2
    kept = kept.reshape((2, size) + kept.shape[1:])
    got = got.reshape(kept.shape)

    def part(which):
        return lax.dynamic_index_in_dim(kept, which, 0, False) + lax.dynamic_index_in_dim(got, which, 0, False)

    return part(1 - mine), part(mine)


def mirror(sums, own, ks, row, others):
    flat = [x for pair in sums for x in pair]
    widths = [pair[0].shape[-1] for pair in sums]
    new = [len(pair) == 2 for pair in sums]
    total = sum(widths)

    def kernel(*refs):
        ins, outs = list(refs[: len(flat)]), list(refs[len(flat) + len(others) :])
        turned_ref = outs.pop()
        at = 0
        for wide, pair in zip(widths, new):
            x = ins.pop(0)
            x = x[0] + ins.pop(0)[0] if pair else x[...]
            if pair:
                outs.pop(0)[...] = x
            turned_ref[at : at + wide, :] = x.T
            at += wide
        if others:
            outs.pop(0)[...] = jnp.concatenate([x[...] for x in reversed(refs[len(flat) : len(flat) + len(others)])], axis=1)
        for k in ks:
            outs.pop(0)[...] = turned_ref[k * own : (k + 1) * own, :]
        if row:
            outs.pop(0)[...] = turned_ref[row : row + 8, :]

    shapes = [f32(own, w) for w, pair in zip(widths, new) if pair] + [f32(own, own * len(others))] * bool(others)
    first = len(shapes)
    shapes += [f32(own, own)] * len(ks) + [f32(8, own)] * bool(row)
    out = list(call(kernel, flat + others, shapes, [pltpu.VMEM((total, own), jnp.float32)]))
    return out[:first], out[first : first + len(ks)], out[-1]


def factor_block(a):
    size = a.shape[0]
    shape = (8, size)
    lane = lax.broadcasted_iota(jnp.int32, shape, 1)
    sub = lax.broadcasted_iota(jnp.int32, shape, 0)
    groups = [a[at : at + 8] for at in range(0, size, 8)]

    def column(x, j):
        return jnp.broadcast_to(x[:, j : j + 1], shape)

    def row(x, s):
        return jnp.broadcast_to(x[s : s + 1, :], shape)

    uppers, lowers = [], []
    for g, x in enumerate(groups):
        first = 8 * g
        inside = (lane >= first) & (lane < first + 8)
        columns = [column(x, first + k) for k in range(8)]
        pivots = jnp.zeros(shape, jnp.float32)
        inverses, rows, cross = [], [], {}
        for k in range(8):
            pivot = row(columns[k], k)
            inverse = pltpu.reciprocal(pivot, approx=True)
            inverse = inverse * (2.0 - pivot * inverse)
            scaled = columns[k] * inverse
            for m in range(k + 1, 8):
                cross[k, m] = row(columns[m], k)
                columns[m] = columns[m] - scaled * cross[k, m]
            at = lane == first + k
            this = jnp.where(at, 1.0, row(x, k))
            x = jnp.where(at & (sub >= k), jnp.where(sub == k, 1.0, 0.0), x) - jnp.where(sub > k, scaled, 0.0) * this
            pivots = jnp.where(sub == k, pivot, pivots)
            inverses.append(inverse)
            rows.append(jnp.where(inside & (lane > first + k), 0.0, this))
        for h in range(g + 1, len(groups)):
            below = groups[h]
            columns = [column(below, first + k) for k in range(8)]
            below = jnp.where(inside, 0.0, below)
            for k in range(8):
                scaled = columns[k] * inverses[k]
                for m in range(k + 1, 8):
                    columns[m] = columns[m] - scaled * cross[k, m]
                below = below - scaled * rows[k]
            groups[h] = below
        root = lax.rsqrt(pivots)
        root = root * (1.5 - 0.5 * pivots * root * root)
        scaled = x * root
        off = lane - first - sub
        uppers.append(jnp.where(off > 0, scaled, jnp.where(off == 0, pivots * root, 0.0)))
        lowers.append(jnp.where(off <= 0, scaled, 0.0))
    return jnp.concatenate(uppers, axis=0).T, jnp.concatenate(lowers, axis=0)


def factor_first_kernel(me_ref, mine_ref, other_ref, damp_ref, g_ref, l11_ref, i11_ref, l21_ref, rest_ref):
    core = me_ref[0] & 1
    half = l11_ref.shape[0]
    rows = half // 2
    mine, other = mine_ref[0], other_ref[0]
    low, high = jnp.where(core == 0, mine, other), jnp.where(core == 0, other, mine)

    def opened(x):
        return jnp.concatenate([x[:, :half], x[:, half:]], axis=0)

    row = lax.broadcasted_iota(jnp.int32, (half, half), 0)
    col = lax.broadcasted_iota(jnp.int32, (half, half), 1)
    n11 = opened(low[:rows]) + jnp.where(row == col, damp_ref[:half, 0:1], 0.0)
    n22 = opened(high[:rows]) + jnp.where(row == col, damp_ref[half:, 0:1], 0.0)
    n21 = jnp.concatenate([opened(x[rows : rows + rows // 2]) for x in (low, high)], axis=0)
    g_ref[...] = mine[rows + rows // 2 : rows + rows // 2 + 8]
    l11, i11 = factor_block(n11)
    l21 = dot_nt(n21, i11, EXACT)
    l11_ref[...] = l11
    i11_ref[...] = i11
    l21_ref[...] = l21
    rest_ref[...] = n22 - dot_nt(l21, l21, EXACT)


def factor_second_kernel(l11_ref, i11_ref, l21_ref, rest_ref, factor_ref, inverse_ref):
    half = l11_ref.shape[0]
    l22, i22 = factor_block(rest_ref[...])
    before = jnp.dot(l21_ref[...], i11_ref[...], precision=EXACT, preferred_element_type=jnp.float32)
    zero = jnp.zeros((half, half), jnp.float32)
    factor_ref[:half, :half] = l11_ref[...]
    factor_ref[:half, half:] = zero
    factor_ref[half:, :half] = l21_ref[...]
    factor_ref[half:, half:] = l22
    inverse_ref[:half, :half] = i11_ref[...]
    inverse_ref[:half, half:] = zero
    inverse_ref[half:, :half] = -jnp.dot(i22, before, precision=EXACT, preferred_element_type=jnp.float32)
    inverse_ref[half:, half:] = i22


def lower_kernel(inverse_ref, g1_ref, held_ref, lower_ref, out_ref, y_ref, flat_ref):
    inverse = inverse_ref[...]
    count, own, size = held_ref.shape
    lower = dot_nt(held_ref[...].reshape(count * own, size), inverse, EXACT).reshape(count, own, size)
    lower_ref[...] = lower
    out_ref[...] = lower[0]
    y = dot_nt(g1_ref[...], inverse, EXACT)
    y_ref[...] = y
    flat_ref[...] = y[0]


def product_kernel(bits, me_ref, mine_ref, other_ref, product_ref, all_ref):
    me = me_ref[0]
    own = product_ref.shape[0]
    for k in range(mine_ref.shape[0]):
        owner = me ^ sum(((k >> i) & 1) << bit for i, bit in enumerate(bits))
        all_ref[pl.ds(pl.multiple_of(owner * own, 16), own), :] = mine_ref[k]
        all_ref[pl.ds(pl.multiple_of((owner ^ 1) * own, 16), own), :] = other_ref[k]
    product_ref[...] = dot_nt(mine_ref[0], all_ref[...], EXACT)


def last_kernel(n_chunks, me_ref, damp_ref, product_ref, g2_ref, y_ref, lower_ref, *refs):
    chunks, mirrors, (schur_ref, rhs_ref) = refs[:n_chunks], refs[n_chunks:-2], refs[-2:]
    rhs_ref[...] = (g2_ref[...] - dot_nt(y_ref[...], lower_ref[...], EXACT))[0]
    me = me_ref[0]
    own = schur_ref.shape[0]
    turned = [m[...] for m in reversed(mirrors)]
    width = schur_ref.shape[1] - sum(x.shape[1] for x in turned)
    whole = jnp.concatenate([c[...] for c in chunks], axis=1)[:, :width]
    row = lax.broadcasted_iota(jnp.int32, (own, own), 0)
    col = lax.broadcasted_iota(jnp.int32, (own, own), 1)
    nat = own * STRIDE // (STRIDE - 1)
    target = lax.broadcasted_iota(jnp.int32, (own, nat), 0)
    target = target + 1 + ((target * 9363) >> 16)
    pick = target == lax.broadcasted_iota(jnp.int32, (own, nat), 1)
    damp = jnp.sum(jnp.where(pick, damp_ref[pl.ds(me, 1), :], 0.0), axis=1, keepdims=True)
    first = whole[:, :own] + jnp.where(row == col, damp, 0.0)
    whole = jnp.concatenate([first, whole[:, own:]] + turned, axis=1)
    schur_ref[...] = pltpu.roll(whole, me * own, 1) - product_ref[...]


def per_device(features, gauge_offset, gauge_count, gauge_resid, damping):
    tiles_here, samples, params = features.shape
    slots = gauge_offset.shape[1]
    axis = "tile"
    n = lax.axis_size(axis)
    panel = params // STRIDE
    trail = params - panel
    own = trail // n
    if n != 16 or own != 112 or params % BLK:
        return per_device_plain(features, gauge_offset, gauge_count, gauge_resid, damping)
    count = n // 2 - 1
    half = n // 2
    widths = (384, 384, 256)
    me = lax.axis_index(axis)
    me1 = me.astype(jnp.int32).reshape(1)
    order = [1, 2, 3]
    orders = [order] * len(widths)
    last = [()]

    def then(*xs):
        xs, last[0] = lax.optimization_barrier((xs, last[0]))
        return xs

    def did(x):
        last[0] = x
        return x

    feats = features.reshape(tiles_here * samples, params)
    sent, p, jt, r = did(front(order, me1, gauge_count, gauge_offset, gauge_resid, feats, half, own))
    p_got = swap(sent, axis, 0)

    def panel_fold(p, got, bit):
        shape = f32(p.shape[0] // 2 + 1, *p.shape[1:])
        sent, p = did(call(functools.partial(panel_fold_kernel, bit), then(me1, p, got), [shape] * 2))
        return p, swap(sent, axis, bit)

    def trail_fold(q, step):
        bit = orders[q][step]
        sent, t[q] = did(fold(*then(t[q], t_got[q]), me, bit))
        t_sent[q] = sent

    def trail_send(q, step):
        t_got[q] = swap(t_sent[q], axis, orders[q][step])

    def trail_step(q, step):
        trail_fold(q, step)
        trail_send(q, step)

    def trail_sum(q):
        kept, got = then(t[q], t_got[q])
        return did(kept[0] + got[0])

    def joined(held, got):
        return did(jnp.concatenate(then(held, got), axis=0))

    p, p_got = panel_fold(p, p_got, order[0])
    out = did(trailing(*then(me1, jt, r), orders, half, own, widths))
    t_sent, t = out[: len(widths)], list(out[len(widths) :])
    t_sent, p_got = lax.optimization_barrier((t_sent, p_got))
    t_sent = list(t_sent)
    t_got = [swap(x, axis, 0) for x in t_sent]
    p, p_got = panel_fold(p, p_got, order[1])
    trail_fold(0, 0)
    p, p_got = panel_fold(p, p_got, order[2])
    t_sent[0] = lax.optimization_barrier((t_sent[0], p))[0]
    trail_send(0, 0)
    trail_step(1, 0)
    trail_step(2, 0)
    damp_panel, damp_trail = then(damping)[0].reshape(panel, STRIDE), damping.reshape(n, params // n)
    damp_panel = did(damp_panel)
    p, p_got = then(p, p_got)
    p = did(p + p_got)
    held, n11 = p[:1], p[1:]
    n11_got = swap(n11, axis, 0)
    got = swap(held, axis, order[2])
    g1, *state = did(
        call(factor_first_kernel, then(me1, n11, n11_got, damp_panel), [f32(8, panel)] + [f32(panel // 2, panel // 2)] * 4)
    )
    trail_step(0, 1)
    held = joined(held, got)
    got = swap(held, axis, order[1])
    trail_step(1, 1)
    factor, inverse = did(call(factor_second_kernel, then(*state), [f32(panel, panel)] * 2))
    trail_step(0, 2)
    held = joined(held, got)
    got = swap(held, axis, order[0])
    trail_step(2, 1)
    trail_step(1, 2)
    first = trail_sum(0)
    trail_step(2, 2)
    held = joined(held, got)
    mine, lower, y, y0 = did(
        call(lower_kernel, then(inverse, g1, held), [f32(half, own, panel), f32(own, panel), f32(8, panel), f32(panel)])
    )
    second = trail_sum(1)
    (third,), blocks, g2 = did(mirror([(first,), (second,), then(t[2], t_got[2])], own, range(1, count + 1), (count + 2) * own, []))
    chunks = [first, second, third]
    mirrors = [lax.ppermute(b, axis, [(i, (i + k) % n) for i in range(n)]) for k, b in enumerate(blocks, 1)]
    other = swap(lax.optimization_barrier((mine, chunks))[0], axis, 0)
    product = did(
        call(
            functools.partial(product_kernel, list(reversed(order))),
            then(me1, mine, other),
            f32(own, trail),
            [pltpu.VMEM((trail, panel), jnp.float32)],
        )
    )
    schur, rhs0 = call(
        functools.partial(last_kernel, len(widths)),
        then(me1, damp_trail, product, g2, y, lower, *chunks, *mirrors),
        [f32(own, trail), f32(own)],
    )
    return (factor, lower, schur, y0, rhs0)


def per_device_plain(features, gauge_offset, gauge_count, gauge_resid, damping):
    tiles_here, samples, params = features.shape
    slots = gauge_offset.shape[1]
    panel = params // 8
    trail = params - panel
    rows_here = tiles_here * slots
    slot_ids = lax.broadcasted_iota(jnp.int32, (tiles_here, slots), 1)
    live = slot_ids < gauge_count[:, None]
    sample_ids = lax.broadcasted_iota(jnp.int32, (tiles_here, slots, samples), 2)
    starts = gauge_offset[:, :, None]
    inside = (sample_ids >= starts) & (sample_ids < starts + LWIN) & live[:, :, None]
    window = jnp.where(inside, 1.0 / LWIN, 0.0).astype(jnp.bfloat16)
    jac = jnp.einsum("tgw,twp->tgp", window, features, preferred_element_type=jnp.float32)
    jac = jac.astype(jnp.bfloat16).reshape(rows_here, params)
    resid = jnp.where(live, gauge_resid, jnp.zeros_like(gauge_resid)).reshape(rows_here)
    grad_local = jnp.dot(resid, jac, preferred_element_type=jnp.float32)
    width = lax.axis_size("tile")
    owned = params // width
    owned_trail = owned - owned // 8
    index = lax.axis_index("tile")
    gauges = jac.shape[0]
    jac_split = jac.reshape(gauges, panel, 8)
    jac_panel = jac_split[:, :, 0]
    jac_trail = jac_split[:, :, 1:].reshape(gauges, trail)
    panel_local = lax.dot_general(jac, jac_panel, (((0,), (0,)), ((), ())), preferred_element_type=jnp.float32)
    panel_all, grad = lax.psum((panel_local, grad_local), "tile")
    own_trail = lax.psum_scatter(
        lax.dot_general(jac_trail, jac_trail, (((0,), (0,)), ((), ())), preferred_element_type=jnp.float32),
        "tile",
        scatter_dimension=0,
        tiled=True,
    )
    damp_split = damping.reshape(panel, 8)
    damp_trail = damp_split[:, 1:].reshape(trail)
    trail_ids = index * owned_trail + lax.broadcasted_iota(jnp.int32, (owned_trail, trail), 0)
    column_ids = lax.broadcasted_iota(jnp.int32, (owned_trail, trail), 1)
    own_trail = own_trail + jnp.where(trail_ids == column_ids, damp_trail[None, :], 0.0)
    panel_split = panel_all.reshape(panel, 8, panel)
    n11 = panel_split[:, 0, :] + jnp.diag(damp_split[:, 0])
    n21 = panel_split[:, 1:, :].reshape(trail, panel)
    panel_factor = jnp.linalg.cholesky(n11)
    lower_all = lax.linalg.triangular_solve(panel_factor, n21, left_side=False, lower=True, transpose_a=True)
    lower_own = lax.dynamic_slice_in_dim(lower_all, index * owned_trail, owned_trail, 0)
    schur = own_trail - jnp.dot(lower_own, lower_all.T, precision=lax.Precision.HIGHEST)
    grad_split = grad.reshape(panel, 8)
    first_part = grad_split[:, 0]
    second_part = grad_split[:, 1:].reshape(trail)
    panel_rhs = lax.linalg.triangular_solve(panel_factor, first_part[:, None], left_side=True, lower=True)[:, 0]
    second_own = lax.dynamic_slice_in_dim(second_part, index * owned_trail, owned_trail, 0)
    trail_rhs = second_own - jnp.dot(lower_own, panel_rhs, precision=lax.Precision.HIGHEST)
    return (panel_factor, lower_own, schur, panel_rhs, trail_rhs)


def solution(mesh):
    return jax.shard_map(
        per_device,
        mesh=mesh,
        in_specs=(
            P(("groups", "tile"), None, None),
            P(("groups", "tile"), None),
            P(("groups", "tile")),
            P(("groups", "tile"), None),
            P("groups"),
        ),
        out_specs=(
            P("groups", None),
            P(("groups", "tile"), None),
            P(("groups", "tile"), None),
            P("groups"),
            P(("groups", "tile")),
        ),
        check_vma=False,
    )
```

```python
import functools

import jax
import jax.numpy as jnp
from jax import lax
from jax.experimental import pallas as pl
from jax.experimental.pallas import tpu as pltpu
from jax.sharding import PartitionSpec as P

LWIN = 8
STRIDE = 8
BLK = 256
EXACT = lax.Precision.HIGHEST
VMEM_LIMIT = 56 * 2**20

SMEM_SPEC = pl.BlockSpec(memory_space=pltpu.SMEM)
VMEM_SPEC = pl.BlockSpec(memory_space=pltpu.VMEM)
NT = (((1,), (1,)), ((), ()))


def f32(*shape):
    return jax.ShapeDtypeStruct(shape, jnp.float32)


def bf16(*shape):
    return jax.ShapeDtypeStruct(shape, jnp.bfloat16)


def dot_nt(a, b, precision=None):
    return lax.dot_general(a, b, NT, precision=precision, preferred_element_type=jnp.float32)


def call(kernel, ins, out_shape, scratch=()):
    return pl.pallas_call(
        kernel,
        out_shape=out_shape,
        in_specs=[SMEM_SPEC if x.dtype == jnp.int32 and x.ndim == 1 else VMEM_SPEC for x in ins],
        out_specs=jax.tree.map(lambda _: VMEM_SPEC, out_shape),
        scratch_shapes=list(scratch),
        compiler_params=pltpu.CompilerParams(vmem_limit_bytes=VMEM_LIMIT),
        cost_estimate=pl.CostEstimate(flops=1, bytes_accessed=1, transcendentals=0),
    )(*ins)


def owner_of(m, order):
    last = len(order) - 1
    return sum(((m >> (last - k)) & 1) << bit for k, bit in enumerate(order))


def front_kernel(
    order, me_ref, count_ref, offset_ref, resid_ref, feat_hbm, sent_hbm, kept_hbm, jt_hbm, r_ref,
    feat_ref, jp_ref, jt_ref, n21_ref, n11_ref, pack_ref, feat_sems, jt_sems, out_sems,
):
    depth, params = feat_ref.shape
    blocks = params // BLK
    core = me_ref[0] & 1
    pan_b = BLK // STRIDE
    trail_b = BLK - pan_b
    feat_copies = [
        pltpu.make_async_copy(feat_hbm.at[:, b * BLK : (b + 1) * BLK], feat_ref.at[:, b * BLK : (b + 1) * BLK], feat_sems.at[b])
        for b in range(blocks)
    ]
    for copy in feat_copies:
        copy.start()
    window, pick = window_part(count_ref, offset_ref, resid_ref, depth, jp_ref.shape[1], r_ref)
    copies = []
    group = blocks // 2
    for b in range(blocks):
        if b % group == 0:
            for copy in feat_copies[b : b + group]:
                copy.wait()
        turned = dot_nt(pick, feat_ref[:, b * BLK : (b + 1) * BLK]).astype(jnp.bfloat16)
        jac = jnp.dot(turned, window, preferred_element_type=jnp.float32).astype(jnp.bfloat16)
        jp_ref[b * pan_b : (b + 1) * pan_b, :] = jac[:pan_b]
        jt_ref[b * trail_b : (b + 1) * trail_b, :] = jac[pan_b:]
        if b % group == group - 1:
            rows = slice((b + 1 - group) * trail_b, (b + 1) * trail_b)
            copies.append(pltpu.make_async_copy(jt_ref.at[rows], jt_hbm.at[rows], jt_sems.at[b // group]))
            copies[-1].start()
    jp = jp_ref[...]
    own, count = sent_hbm.shape[1], sent_hbm.shape[0] - 1
    ways = ((sent_hbm, 1 - core), (kept_hbm, core))
    panel = jp.shape[0]
    half, part = panel // 2, panel // 4
    n11_ref[...] = dot_nt(jp, jp)
    grad = dot_nt(r_ref[...], jp)
    for k, (out, which) in enumerate(ways):
        for side in range(2):
            lanes = slice(side * half, (side + 1) * half)
            at = pl.multiple_of(which * half + side * part, 16)
            first = n11_ref[pl.ds(at, part), :]
            pack_ref[k, :part, lanes] = jnp.where(which == 1, first[:, half:], first[:, :half])
            at = pl.multiple_of(half + which * part + side * (part // 2), 16)
            pack_ref[k, part : part + part // 2, lanes] = n11_ref[pl.ds(at, part // 2), :half]
        pack_ref[k, part + part // 2 :, :] = grad[: own - part - part // 2]
        copies.append(pltpu.make_async_copy(pack_ref.at[k], out.at[count], out_sems.at[k, count]))
        copies[-1].start()
    for first in range(0, count, count // 4):
        rows = slice(first * 2 * own, (first + count // 4) * 2 * own)
        n21_ref[rows, :] = dot_nt(jt_ref[rows, :], jp)
        for m in range(first, first + count // 4):
            for k, (out, which) in enumerate(ways):
                source = n21_ref.at[pl.ds(pl.multiple_of(m * 2 * own + which * own, 16), own), :]
                copies.append(pltpu.make_async_copy(source, out.at[place_of(m, order)], out_sems.at[k, m]))
                copies[-1].start()
    for copy in copies:
        copy.wait()


def window_part(count_ref, offset_ref, resid_ref, depth, cap, r_ref):
    tiles, slots = offset_ref.shape
    samples = depth // tiles
    lane = lax.broadcasted_iota(jnp.int32, (8, cap), 1)
    row = lax.broadcasted_iota(jnp.int32, (8, slots), 0)
    merged = jnp.where(lax.broadcasted_iota(jnp.int32, (8, cap), 0) == 0, -1.0 * depth, 0.0)
    before = jnp.int32(0)
    for t in range(tiles):
        count = count_ref[t]
        live = (lane >= before) & (lane < before + count)
        offs = (offset_ref[t : t + 1, :] + t * samples).astype(jnp.float32)
        both = jnp.where(row == 0, offs, jnp.where(row == 1, resid_ref[t : t + 1, :].astype(jnp.float32), 0.0))
        both = jnp.concatenate([both, jnp.zeros((8, cap - slots), jnp.float32)], axis=1)
        merged = jnp.where(live, pltpu.roll(both, before, 1), merged)
        before = before + count
    start = merged[0:1].astype(jnp.int32)
    r_ref[...] = jnp.concatenate([merged[1:], jnp.zeros((9, cap), jnp.float32)], axis=0).astype(jnp.bfloat16)
    after = lax.broadcasted_iota(jnp.int32, (depth, cap), 0) - start
    window = jnp.where((after >= 0) & (after < LWIN), 1.0 / LWIN, 0.0).astype(jnp.bfloat16)
    pan_b = BLK // STRIDE
    row = lax.broadcasted_iota(jnp.int32, (BLK, BLK), 0)
    col = lax.broadcasted_iota(jnp.int32, (BLK, BLK), 1)
    rest = row - pan_b
    source = jnp.where(row < pan_b, row * STRIDE, rest + 1 + ((rest * 9363) >> 16))
    return window, jnp.where(source == col, 1.0, 0.0).astype(jnp.bfloat16)


def trail_kernel(me_ref, jt_hbm, r_ref, *refs):
    outs, (pair_ref, jt_ref, sems) = refs[:-3], refs[-3:]
    sent, kept = outs[: len(outs) // 2], outs[len(outs) // 2 :]
    m = pl.program_id(0)
    core = me_ref[0] & 1
    own = sent[0].shape[1]
    base = m * 2 * own
    pairs = jt_hbm.shape[0] // (2 * own)
    ahead = jt_ref.shape[0] // (2 * own) - pairs

    def brought(k):
        source = jt_hbm.at[pl.ds(pl.multiple_of(lax.rem(k, pairs) * 2 * own, 16), 2 * own), :]
        return pltpu.make_async_copy(source, jt_ref.at[pl.ds(pl.multiple_of(k * 2 * own, 16), 2 * own), :], sems.at[k])

    @pl.when(m == 0)
    def _():
        for k in range(pairs + ahead):
            brought(jnp.int32(k)).start()
        for k in range(ahead):
            brought(jnp.int32(k)).wait()

    brought(m + ahead).wait()
    real = pair_ref.shape[2] - r_ref.shape[0]
    rows = jt_ref[pl.ds(pl.multiple_of(base, 16), 2 * own), :]
    others = jt_ref[pl.ds(pl.multiple_of(base, 16), real + own), :]
    both = dot_nt(rows, others)
    last = dot_nt(rows, r_ref[...])
    pair_ref[0, :, :real] = both[:own, :real]
    pair_ref[0, :, real:] = last[:own]
    pair_ref[1, :, :real] = both[own:, own:]
    pair_ref[1, :, real:] = last[own:]
    for group, which in ((sent, 1 - core), (kept, core)):
        at = 0
        for ref in group:
            ref[0] = pair_ref[which, :, at : at + ref.shape[2]]
            at += ref.shape[2]


def place_of(m, order):
    return sum(((m >> (bit - 1)) & 1) << (len(order) - 1 - k) for k, bit in enumerate(order))


def trailing(me1, jt, r, orders, half, own, widths):
    def spec(order, wide):
        return pl.BlockSpec((1, own, wide), lambda m: (place_of(m, order), 0, 0))

    pairs = half + half // 2
    return pl.pallas_call(
        trail_kernel,
        grid=(half,),
        out_shape=[f32(half, own, wide) for wide in widths] * 2,
        in_specs=[SMEM_SPEC, pl.BlockSpec(memory_space=pl.ANY), pl.BlockSpec(r.shape, lambda m: (0, 0))],
        out_specs=[spec(order, wide) for order, wide in zip(orders, widths)] * 2,
        scratch_shapes=[
            pltpu.VMEM((2, own, sum(widths)), jnp.float32),
            pltpu.VMEM((2 * own * pairs, jt.shape[1]), jnp.bfloat16),
            pltpu.SemaphoreType.DMA((pairs,)),
        ],
        compiler_params=pltpu.CompilerParams(vmem_limit_bytes=VMEM_LIMIT),
        cost_estimate=pl.CostEstimate(flops=1, bytes_accessed=1, transcendentals=0),
    )(me1, jt, r)


def front(order, me1, gauge_count, gauge_offset, gauge_resid, feats, half, own):
    depth, params = feats.shape
    cap = gauge_offset.size // 2
    panel = params // STRIDE
    trail = params - panel
    hbm = pl.BlockSpec(memory_space=pl.ANY)
    return pl.pallas_call(
        functools.partial(front_kernel, order),
        out_shape=[f32(half + 1, own, panel)] * 2 + [bf16(trail, cap), bf16(16, cap)],
        in_specs=[SMEM_SPEC, SMEM_SPEC, VMEM_SPEC, VMEM_SPEC, hbm],
        out_specs=[hbm, hbm, hbm, VMEM_SPEC],
        scratch_shapes=[
            pltpu.VMEM((depth, params), jnp.bfloat16),
            pltpu.VMEM((panel, cap), jnp.bfloat16),
            pltpu.VMEM((trail, cap), jnp.bfloat16),
            pltpu.VMEM((trail, panel), jnp.float32),
            pltpu.VMEM((panel, panel), jnp.float32),
            pltpu.VMEM((2, own, panel), jnp.float32),
            pltpu.SemaphoreType.DMA((params // BLK,)),
            pltpu.SemaphoreType.DMA((2,)),
            pltpu.SemaphoreType.DMA((2, half + 1)),
        ],
        compiler_params=pltpu.CompilerParams(vmem_limit_bytes=VMEM_LIMIT),
        cost_estimate=pl.CostEstimate(flops=1, bytes_accessed=1, transcendentals=0),
    )(me1, gauge_count, gauge_offset, gauge_resid, feats)


def swap(x, axis, bit):
    n = lax.axis_size(axis)
    return lax.ppermute(x, axis, [(i, i ^ (1 << bit)) for i in range(n)])


def panel_fold_kernel(bit, me_ref, kept_ref, got_ref, sent_out, kept_out):
    mine = (me_ref[0] >> bit) & 1
    size = kept_out.shape[0] - 1
    for k in range(size):
        sent_out[k] = kept_ref[(1 - mine) * size + k] + got_ref[(1 - mine) * size + k]
        kept_out[k] = kept_ref[mine * size + k] + got_ref[mine * size + k]
    total = kept_ref[2 * size] + got_ref[2 * size]
    sent_out[size] = total
    kept_out[size] = total


def fold(kept, got, me, bit):
    mine = (me >> bit) & 1
    size = kept.shape[0] // 2
    kept = kept.reshape((2, size) + kept.shape[1:])
    got = got.reshape(kept.shape)

    def part(which):
        return lax.dynamic_index_in_dim(kept, which, 0, False) + lax.dynamic_index_in_dim(got, which, 0, False)

    return part(1 - mine), part(mine)


def mirror(sums, own, ks, row, others):
    flat = [x for pair in sums for x in pair]
    widths = [pair[0].shape[-1] for pair in sums]
    new = [len(pair) == 2 for pair in sums]
    total = sum(widths)

    def kernel(*refs):
        ins, outs = list(refs[: len(flat)]), list(refs[len(flat) + len(others) :])
        turned_ref = outs.pop()
        at = 0
        for wide, pair in zip(widths, new):
            x = ins.pop(0)
            x = x[0] + ins.pop(0)[0] if pair else x[...]
            if pair:
                outs.pop(0)[...] = x
            turned_ref[at : at + wide, :] = x.T
            at += wide
        if others:
            outs.pop(0)[...] = jnp.concatenate([x[...] for x in reversed(refs[len(flat) : len(flat) + len(others)])], axis=1)
        for k in ks:
            outs.pop(0)[...] = turned_ref[k * own : (k + 1) * own, :]
        if row:
            outs.pop(0)[...] = turned_ref[row : row + 8, :]

    shapes = [f32(own, w) for w, pair in zip(widths, new) if pair] + [f32(own, own * len(others))] * bool(others)
    first = len(shapes)
    shapes += [f32(own, own)] * len(ks) + [f32(8, own)] * bool(row)
    out = list(call(kernel, flat + others, shapes, [pltpu.VMEM((total, own), jnp.float32)]))
    return out[:first], out[first : first + len(ks)], out[-1]


def factor_block(a):
    size = a.shape[0]
    shape = (8, size)
    lane = lax.broadcasted_iota(jnp.int32, shape, 1)
    sub = lax.broadcasted_iota(jnp.int32, shape, 0)
    groups = [a[at : at + 8] for at in range(0, size, 8)]

    def column(x, j):
        return jnp.broadcast_to(x[:, j : j + 1], shape)

    def row(x, s):
        return jnp.broadcast_to(x[s : s + 1, :], shape)

    uppers, lowers = [], []
    for g, x in enumerate(groups):
        first = 8 * g
        inside = (lane >= first) & (lane < first + 8)
        columns = [column(x, first + k) for k in range(8)]
        pivots = jnp.zeros(shape, jnp.float32)
        inverses, rows, cross = [], [], {}
        for k in range(8):
            pivot = row(columns[k], k)
            inverse = pltpu.reciprocal(pivot, approx=True)
            inverse = inverse * (2.0 - pivot * inverse)
            scaled = columns[k] * inverse
            for m in range(k + 1, 8):
                cross[k, m] = row(columns[m], k)
                columns[m] = columns[m] - scaled * cross[k, m]
            at = lane == first + k
            this = jnp.where(at, 1.0, row(x, k))
            x = jnp.where(at & (sub >= k), jnp.where(sub == k, 1.0, 0.0), x) - jnp.where(sub > k, scaled, 0.0) * this
            pivots = jnp.where(sub == k, pivot, pivots)
            inverses.append(inverse)
            rows.append(jnp.where(inside & (lane > first + k), 0.0, this))
        for h in range(g + 1, len(groups)):
            below = groups[h]
            columns = [column(below, first + k) for k in range(8)]
            below = jnp.where(inside, 0.0, below)
            for k in range(8):
                scaled = columns[k] * inverses[k]
                for m in range(k + 1, 8):
                    columns[m] = columns[m] - scaled * cross[k, m]
                below = below - scaled * rows[k]
            groups[h] = below
        root = lax.rsqrt(pivots)
        root = root * (1.5 - 0.5 * pivots * root * root)
        scaled = x * root
        off = lane - first - sub
        uppers.append(jnp.where(off > 0, scaled, jnp.where(off == 0, pivots * root, 0.0)))
        lowers.append(jnp.where(off <= 0, scaled, 0.0))
    return jnp.concatenate(uppers, axis=0).T, jnp.concatenate(lowers, axis=0)


def factor_first_kernel(me_ref, mine_ref, other_ref, damp_ref, g_ref, l11_ref, i11_ref, l21_ref, rest_ref):
    core = me_ref[0] & 1
    half = l11_ref.shape[0]
    rows = half // 2
    mine, other = mine_ref[0], other_ref[0]
    low, high = jnp.where(core == 0, mine, other), jnp.where(core == 0, other, mine)

    def opened(x):
        return jnp.concatenate([x[:, :half], x[:, half:]], axis=0)

    row = lax.broadcasted_iota(jnp.int32, (half, half), 0)
    col = lax.broadcasted_iota(jnp.int32, (half, half), 1)
    n11 = opened(low[:rows]) + jnp.where(row == col, damp_ref[:half, 0:1], 0.0)
    n22 = opened(high[:rows]) + jnp.where(row == col, damp_ref[half:, 0:1], 0.0)
    n21 = jnp.concatenate([opened(x[rows : rows + rows // 2]) for x in (low, high)], axis=0)
    g_ref[...] = mine[rows + rows // 2 : rows + rows // 2 + 8]
    l11, i11 = factor_block(n11)
    l21 = dot_nt(n21, i11, EXACT)
    l11_ref[...] = l11
    i11_ref[...] = i11
    l21_ref[...] = l21
    rest_ref[...] = n22 - dot_nt(l21, l21, EXACT)


def factor_second_kernel(l11_ref, i11_ref, l21_ref, rest_ref, factor_ref, inverse_ref):
    half = l11_ref.shape[0]
    l22, i22 = factor_block(rest_ref[...])
    before = jnp.dot(l21_ref[...], i11_ref[...], precision=EXACT, preferred_element_type=jnp.float32)
    zero = jnp.zeros((half, half), jnp.float32)
    factor_ref[:half, :half] = l11_ref[...]
    factor_ref[:half, half:] = zero
    factor_ref[half:, :half] = l21_ref[...]
    factor_ref[half:, half:] = l22
    inverse_ref[:half, :half] = i11_ref[...]
    inverse_ref[:half, half:] = zero
    inverse_ref[half:, :half] = -jnp.dot(i22, before, precision=EXACT, preferred_element_type=jnp.float32)
    inverse_ref[half:, half:] = i22


def lower_kernel(inverse_ref, g1_ref, held_ref, lower_ref, out_ref, y_ref, flat_ref):
    inverse = inverse_ref[...]
    count, own, size = held_ref.shape
    lower = dot_nt(held_ref[...].reshape(count * own, size), inverse, EXACT).reshape(count, own, size)
    lower_ref[...] = lower
    out_ref[...] = lower[0]
    y = dot_nt(g1_ref[...], inverse, EXACT)
    y_ref[...] = y
    flat_ref[...] = y[0]


def product_kernel(bits, me_ref, mine_ref, other_ref, product_ref, all_ref):
    me = me_ref[0]
    own = product_ref.shape[0]
    for k in range(mine_ref.shape[0]):
        owner = me ^ sum(((k >> i) & 1) << bit for i, bit in enumerate(bits))
        all_ref[pl.ds(pl.multiple_of(owner * own, 16), own), :] = mine_ref[k]
        all_ref[pl.ds(pl.multiple_of((owner ^ 1) * own, 16), own), :] = other_ref[k]
    product_ref[...] = dot_nt(mine_ref[0], all_ref[...], EXACT)


def last_kernel(n_chunks, me_ref, damp_ref, product_ref, g2_ref, y_ref, lower_ref, *refs):
    chunks, mirrors, (schur_ref, rhs_ref) = refs[:n_chunks], refs[n_chunks:-2], refs[-2:]
    rhs_ref[...] = (g2_ref[...] - dot_nt(y_ref[...], lower_ref[...], EXACT))[0]
    me = me_ref[0]
    own = schur_ref.shape[0]
    turned = [m[...] for m in reversed(mirrors[1:])] + [mirrors[0][...]]
    width = schur_ref.shape[1] - sum(x.shape[1] for x in turned)
    whole = jnp.concatenate([c[...] for c in chunks], axis=1)[:, :width]
    row = lax.broadcasted_iota(jnp.int32, (own, own), 0)
    col = lax.broadcasted_iota(jnp.int32, (own, own), 1)
    nat = own * STRIDE // (STRIDE - 1)
    target = lax.broadcasted_iota(jnp.int32, (own, nat), 0)
    target = target + 1 + ((target * 9363) >> 16)
    pick = target == lax.broadcasted_iota(jnp.int32, (own, nat), 1)
    damp = jnp.sum(jnp.where(pick, damp_ref[pl.ds(me, 1), :], 0.0), axis=1, keepdims=True)
    first = whole[:, :own] + jnp.where(row == col, damp, 0.0)
    whole = jnp.concatenate([first, whole[:, own:]] + turned, axis=1)
    schur_ref[...] = pltpu.roll(whole, me * own, 1) - product_ref[...]


def per_device(features, gauge_offset, gauge_count, gauge_resid, damping):
    tiles_here, samples, params = features.shape
    slots = gauge_offset.shape[1]
    axis = "tile"
    n = lax.axis_size(axis)
    panel = params // STRIDE
    trail = params - panel
    own = trail // n
    if n != 16 or own != 112 or params % BLK:
        return per_device_plain(features, gauge_offset, gauge_count, gauge_resid, damping)
    count = n // 2 - 1
    half = n // 2
    widths = (384, 384, 256)
    me = lax.axis_index(axis)
    me1 = me.astype(jnp.int32).reshape(1)
    order = [1, 2, 3]
    orders = [order] * len(widths)
    last = [()]

    def then(*xs):
        xs, last[0] = lax.optimization_barrier((xs, last[0]))
        return xs

    def did(x):
        last[0] = x
        return x

    feats = features.reshape(tiles_here * samples, params)
    sent, p, jt, r = did(front(order, me1, gauge_count, gauge_offset, gauge_resid, feats, half, own))
    p_got = swap(sent, axis, 0)

    def panel_fold(p, got, bit):
        shape = f32(p.shape[0] // 2 + 1, *p.shape[1:])
        sent, p = did(call(functools.partial(panel_fold_kernel, bit), then(me1, p, got), [shape] * 2))
        return p, swap(sent, axis, bit)

    def trail_fold(q, step):
        bit = orders[q][step]
        sent, t[q] = did(fold(*then(t[q], t_got[q]), me, bit))
        t_sent[q] = sent

    def trail_send(q, step):
        t_got[q] = swap(t_sent[q], axis, orders[q][step])

    def trail_step(q, step):
        trail_fold(q, step)
        trail_send(q, step)

    def trail_sum(q):
        kept, got = then(t[q], t_got[q])
        return did(kept[0] + got[0])

    def joined(held, got):
        return did(jnp.concatenate(then(held, got), axis=0))

    p, p_got = panel_fold(p, p_got, order[0])
    out = did(trailing(*then(me1, jt, r), orders, half, own, widths))
    t_sent, t = out[: len(widths)], list(out[len(widths) :])
    t_sent, p_got = lax.optimization_barrier((t_sent, p_got))
    t_sent = list(t_sent)
    t_got = [swap(x, axis, 0) for x in t_sent]
    p, p_got = panel_fold(p, p_got, order[1])
    trail_step(0, 0)
    p, p_got = panel_fold(p, p_got, order[2])
    trail_step(1, 0)
    trail_step(2, 0)
    damp_panel, damp_trail = then(damping)[0].reshape(panel, STRIDE), damping.reshape(n, params // n)
    damp_panel = did(damp_panel)
    p, p_got = then(p, p_got)
    p = did(p + p_got)
    held, n11 = p[:1], p[1:]
    n11_got = swap(n11, axis, 0)
    got = swap(held, axis, order[2])
    trail_step(0, 1)
    g1, *state = did(
        call(factor_first_kernel, then(me1, n11, n11_got, damp_panel), [f32(8, panel)] + [f32(panel // 2, panel // 2)] * 4)
    )
    held = joined(held, got)
    got = swap(held, axis, order[1])
    trail_step(0, 2)
    trail_step(1, 1)
    factor, inverse = did(call(factor_second_kernel, then(*state), [f32(panel, panel)] * 2))
    held = joined(held, got)
    got = swap(held, axis, order[0])
    trail_step(2, 1)
    trail_step(1, 2)
    first = trail_sum(0)
    near = widths[0] // own
    _, blocks, _ = did(mirror([then(first)], own, range(1, near), 0, []))

    def mirrored(blocks, ks):
        return [lax.ppermute(b, axis, [(i, (i + k) % n) for i in range(n)]) for k, b in zip(ks, blocks)]

    near_mirrors = mirrored(blocks, range(1, near))
    trail_step(2, 2)
    held = joined(held, got)
    mine, lower, y, y0 = did(
        call(lower_kernel, then(inverse, g1, held), [f32(half, own, panel), f32(own, panel), f32(8, panel), f32(panel)])
    )
    second = trail_sum(1)
    (third, right), blocks, g2 = did(
        mirror([(first,), (second,), then(t[2], t_got[2])], own, range(near, count + 1), (count + 2) * own, near_mirrors)
    )
    chunks = [first, second, third]
    mirrors = mirrored(blocks, range(near, count + 1))
    other = swap(lax.optimization_barrier((mine, chunks))[0], axis, 0)
    product = did(
        call(
            functools.partial(product_kernel, list(reversed(order))),
            then(me1, mine, other),
            f32(own, trail),
            [pltpu.VMEM((trail, panel), jnp.float32)],
        )
    )
    schur, rhs0 = call(
        functools.partial(last_kernel, len(widths)),
        then(me1, damp_trail, product, g2, y, lower, *chunks, right, *mirrors),
        [f32(own, trail), f32(own)],
    )
    return (factor, lower, schur, y0, rhs0)


def per_device_plain(features, gauge_offset, gauge_count, gauge_resid, damping):
    tiles_here, samples, params = features.shape
    slots = gauge_offset.shape[1]
    panel = params // 8
    trail = params - panel
    rows_here = tiles_here * slots
    slot_ids = lax.broadcasted_iota(jnp.int32, (tiles_here, slots), 1)
    live = slot_ids < gauge_count[:, None]
    sample_ids = lax.broadcasted_iota(jnp.int32, (tiles_here, slots, samples), 2)
    starts = gauge_offset[:, :, None]
    inside = (sample_ids >= starts) & (sample_ids < starts + LWIN) & live[:, :, None]
    window = jnp.where(inside, 1.0 / LWIN, 0.0).astype(jnp.bfloat16)
    jac = jnp.einsum("tgw,twp->tgp", window, features, preferred_element_type=jnp.float32)
    jac = jac.astype(jnp.bfloat16).reshape(rows_here, params)
    resid = jnp.where(live, gauge_resid, jnp.zeros_like(gauge_resid)).reshape(rows_here)
    grad_local = jnp.dot(resid, jac, preferred_element_type=jnp.float32)
    width = lax.axis_size("tile")
    owned = params // width
    owned_trail = owned - owned // 8
    index = lax.axis_index("tile")
    gauges = jac.shape[0]
    jac_split = jac.reshape(gauges, panel, 8)
    jac_panel = jac_split[:, :, 0]
    jac_trail = jac_split[:, :, 1:].reshape(gauges, trail)
    panel_local = lax.dot_general(jac, jac_panel, (((0,), (0,)), ((), ())), preferred_element_type=jnp.float32)
    panel_all, grad = lax.psum((panel_local, grad_local), "tile")
    own_trail = lax.psum_scatter(
        lax.dot_general(jac_trail, jac_trail, (((0,), (0,)), ((), ())), preferred_element_type=jnp.float32),
        "tile",
        scatter_dimension=0,
        tiled=True,
    )
    damp_split = damping.reshape(panel, 8)
    damp_trail = damp_split[:, 1:].reshape(trail)
    trail_ids = index * owned_trail + lax.broadcasted_iota(jnp.int32, (owned_trail, trail), 0)
    column_ids = lax.broadcasted_iota(jnp.int32, (owned_trail, trail), 1)
    own_trail = own_trail + jnp.where(trail_ids == column_ids, damp_trail[None, :], 0.0)
    panel_split = panel_all.reshape(panel, 8, panel)
    n11 = panel_split[:, 0, :] + jnp.diag(damp_split[:, 0])
    n21 = panel_split[:, 1:, :].reshape(trail, panel)
    panel_factor = jnp.linalg.cholesky(n11)
    lower_all = lax.linalg.triangular_solve(panel_factor, n21, left_side=False, lower=True, transpose_a=True)
    lower_own = lax.dynamic_slice_in_dim(lower_all, index * owned_trail, owned_trail, 0)
    schur = own_trail - jnp.dot(lower_own, lower_all.T, precision=lax.Precision.HIGHEST)
    grad_split = grad.reshape(panel, 8)
    first_part = grad_split[:, 0]
    second_part = grad_split[:, 1:].reshape(trail)
    panel_rhs = lax.linalg.triangular_solve(panel_factor, first_part[:, None], left_side=True, lower=True)[:, 0]
    second_own = lax.dynamic_slice_in_dim(second_part, index * owned_trail, owned_trail, 0)
    trail_rhs = second_own - jnp.dot(lower_own, panel_rhs, precision=lax.Precision.HIGHEST)
    return (panel_factor, lower_own, schur, panel_rhs, trail_rhs)


def solution(mesh):
    return jax.shard_map(
        per_device,
        mesh=mesh,
        in_specs=(
            P(("groups", "tile"), None, None),
            P(("groups", "tile"), None),
            P(("groups", "tile")),
            P(("groups", "tile"), None),
            P("groups"),
        ),
        out_specs=(
            P("groups", None),
            P(("groups", "tile"), None),
            P(("groups", "tile"), None),
            P("groups"),
            P(("groups", "tile")),
        ),
        check_vma=False,
    )
```

```python
import functools

import jax
import jax.numpy as jnp
from jax import lax
from jax.experimental import pallas as pl
from jax.experimental.pallas import tpu as pltpu
from jax.sharding import PartitionSpec as P

LWIN = 8
STRIDE = 8
BLK = 256
EXACT = lax.Precision.HIGHEST
VMEM_LIMIT = 56 * 2**20

SMEM_SPEC = pl.BlockSpec(memory_space=pltpu.SMEM)
VMEM_SPEC = pl.BlockSpec(memory_space=pltpu.VMEM)
NT = (((1,), (1,)), ((), ()))


def f32(*shape):
    return jax.ShapeDtypeStruct(shape, jnp.float32)


def bf16(*shape):
    return jax.ShapeDtypeStruct(shape, jnp.bfloat16)


def dot_nt(a, b, precision=None):
    return lax.dot_general(a, b, NT, precision=precision, preferred_element_type=jnp.float32)


def call(kernel, ins, out_shape, scratch=()):
    return pl.pallas_call(
        kernel,
        out_shape=out_shape,
        in_specs=[SMEM_SPEC if x.dtype == jnp.int32 and x.ndim == 1 else VMEM_SPEC for x in ins],
        out_specs=jax.tree.map(lambda _: VMEM_SPEC, out_shape),
        scratch_shapes=list(scratch),
        compiler_params=pltpu.CompilerParams(vmem_limit_bytes=VMEM_LIMIT),
        cost_estimate=pl.CostEstimate(flops=1, bytes_accessed=1, transcendentals=0),
    )(*ins)


def owner_of(m, order):
    last = len(order) - 1
    return sum(((m >> (last - k)) & 1) << bit for k, bit in enumerate(order))


def front_kernel(
    order, me_ref, count_ref, offset_ref, resid_ref, feat_hbm, sent_hbm, kept_hbm, jt_hbm, r_ref,
    feat_ref, jp_ref, jt_ref, n21_ref, n11_ref, pack_ref, feat_sems, jt_sems, out_sems,
):
    depth, params = feat_ref.shape
    blocks = params // BLK
    core = me_ref[0] & 1
    pan_b = BLK // STRIDE
    trail_b = BLK - pan_b
    feat_copies = [
        pltpu.make_async_copy(feat_hbm.at[:, b * BLK : (b + 1) * BLK], feat_ref.at[:, b * BLK : (b + 1) * BLK], feat_sems.at[b])
        for b in range(blocks)
    ]
    for copy in feat_copies:
        copy.start()
    window, pick = window_part(count_ref, offset_ref, resid_ref, depth, jp_ref.shape[1], r_ref)
    copies = []
    group = blocks // 2
    for b in range(blocks):
        if b % group == 0:
            for copy in feat_copies[b : b + group]:
                copy.wait()
        turned = dot_nt(pick, feat_ref[:, b * BLK : (b + 1) * BLK]).astype(jnp.bfloat16)
        jac = jnp.dot(turned, window, preferred_element_type=jnp.float32).astype(jnp.bfloat16)
        jp_ref[b * pan_b : (b + 1) * pan_b, :] = jac[:pan_b]
        jt_ref[b * trail_b : (b + 1) * trail_b, :] = jac[pan_b:]
        if b % group == group - 1:
            rows = slice((b + 1 - group) * trail_b, (b + 1) * trail_b)
            copies.append(pltpu.make_async_copy(jt_ref.at[rows], jt_hbm.at[rows], jt_sems.at[b // group]))
            copies[-1].start()
    jp = jp_ref[...]
    own, count = sent_hbm.shape[1], sent_hbm.shape[0] - 1
    ways = ((sent_hbm, 1 - core), (kept_hbm, core))
    panel = jp.shape[0]
    half, part = panel // 2, panel // 4
    n11_ref[...] = dot_nt(jp, jp)
    grad = dot_nt(r_ref[...], jp)
    for k, (out, which) in enumerate(ways):
        for side in range(2):
            lanes = slice(side * half, (side + 1) * half)
            at = pl.multiple_of(which * half + side * part, 16)
            first = n11_ref[pl.ds(at, part), :]
            pack_ref[k, :part, lanes] = jnp.where(which == 1, first[:, half:], first[:, :half])
            at = pl.multiple_of(half + which * part + side * (part // 2), 16)
            pack_ref[k, part : part + part // 2, lanes] = n11_ref[pl.ds(at, part // 2), :half]
        pack_ref[k, part + part // 2 :, :] = grad[: own - part - part // 2]
        copies.append(pltpu.make_async_copy(pack_ref.at[k], out.at[count], out_sems.at[k, count]))
        copies[-1].start()
    for first in range(0, count, count // 4):
        rows = slice(first * 2 * own, (first + count // 4) * 2 * own)
        n21_ref[rows, :] = dot_nt(jt_ref[rows, :], jp)
        for m in range(first, first + count // 4):
            for k, (out, which) in enumerate(ways):
                source = n21_ref.at[pl.ds(pl.multiple_of(m * 2 * own + which * own, 16), own), :]
                copies.append(pltpu.make_async_copy(source, out.at[place_of(m, order)], out_sems.at[k, m]))
                copies[-1].start()
    for copy in copies:
        copy.wait()


def window_part(count_ref, offset_ref, resid_ref, depth, cap, r_ref):
    tiles, slots = offset_ref.shape
    samples = depth // tiles
    lane = lax.broadcasted_iota(jnp.int32, (8, cap), 1)
    row = lax.broadcasted_iota(jnp.int32, (8, slots), 0)
    merged = jnp.where(lax.broadcasted_iota(jnp.int32, (8, cap), 0) == 0, -1.0 * depth, 0.0)
    before = jnp.int32(0)
    for t in range(tiles):
        count = count_ref[t]
        live = (lane >= before) & (lane < before + count)
        offs = (offset_ref[t : t + 1, :] + t * samples).astype(jnp.float32)
        both = jnp.where(row == 0, offs, jnp.where(row == 1, resid_ref[t : t + 1, :].astype(jnp.float32), 0.0))
        both = jnp.concatenate([both, jnp.zeros((8, cap - slots), jnp.float32)], axis=1)
        merged = jnp.where(live, pltpu.roll(both, before, 1), merged)
        before = before + count
    start = merged[0:1].astype(jnp.int32)
    r_ref[...] = jnp.concatenate([merged[1:], jnp.zeros((9, cap), jnp.float32)], axis=0).astype(jnp.bfloat16)
    after = lax.broadcasted_iota(jnp.int32, (depth, cap), 0) - start
    window = jnp.where((after >= 0) & (after < LWIN), 1.0 / LWIN, 0.0).astype(jnp.bfloat16)
    pan_b = BLK // STRIDE
    row = lax.broadcasted_iota(jnp.int32, (BLK, BLK), 0)
    col = lax.broadcasted_iota(jnp.int32, (BLK, BLK), 1)
    rest = row - pan_b
    source = jnp.where(row < pan_b, row * STRIDE, rest + 1 + ((rest * 9363) >> 16))
    return window, jnp.where(source == col, 1.0, 0.0).astype(jnp.bfloat16)


def trail_kernel(me_ref, jt_hbm, r_ref, *refs):
    outs, (pair_ref, jt_ref, sems) = refs[:-3], refs[-3:]
    sent, kept = outs[: len(outs) // 2], outs[len(outs) // 2 :]
    m = pl.program_id(0)
    core = me_ref[0] & 1
    own = sent[0].shape[1]
    base = m * 2 * own
    pairs = jt_hbm.shape[0] // (2 * own)
    ahead = jt_ref.shape[0] // (2 * own) - pairs

    def brought(k):
        source = jt_hbm.at[pl.ds(pl.multiple_of(lax.rem(k, pairs) * 2 * own, 16), 2 * own), :]
        return pltpu.make_async_copy(source, jt_ref.at[pl.ds(pl.multiple_of(k * 2 * own, 16), 2 * own), :], sems.at[k])

    @pl.when(m == 0)
    def _():
        for k in range(pairs + ahead):
            brought(jnp.int32(k)).start()
        for k in range(ahead):
            brought(jnp.int32(k)).wait()

    brought(m + ahead).wait()
    real = pair_ref.shape[2] - r_ref.shape[0]
    rows = jt_ref[pl.ds(pl.multiple_of(base, 16), 2 * own), :]
    others = jt_ref[pl.ds(pl.multiple_of(base, 16), real + own), :]
    both = dot_nt(rows, others)
    last = dot_nt(rows, r_ref[...])
    pair_ref[0, :, :real] = both[:own, :real]
    pair_ref[0, :, real:] = last[:own]
    pair_ref[1, :, :real] = both[own:, own:]
    pair_ref[1, :, real:] = last[own:]
    for group, which in ((sent, 1 - core), (kept, core)):
        at = 0
        for ref in group:
            ref[0] = pair_ref[which, :, at : at + ref.shape[2]]
            at += ref.shape[2]


def place_of(m, order):
    return sum(((m >> (bit - 1)) & 1) << (len(order) - 1 - k) for k, bit in enumerate(order))


def trailing(me1, jt, r, orders, half, own, widths):
    def spec(order, wide):
        return pl.BlockSpec((1, own, wide), lambda m: (place_of(m, order), 0, 0))

    pairs = half + half // 2
    return pl.pallas_call(
        trail_kernel,
        grid=(half,),
        out_shape=[f32(half, own, wide) for wide in widths] * 2,
        in_specs=[SMEM_SPEC, pl.BlockSpec(memory_space=pl.ANY), pl.BlockSpec(r.shape, lambda m: (0, 0))],
        out_specs=[spec(order, wide) for order, wide in zip(orders, widths)] * 2,
        scratch_shapes=[
            pltpu.VMEM((2, own, sum(widths)), jnp.float32),
            pltpu.VMEM((2 * own * pairs, jt.shape[1]), jnp.bfloat16),
            pltpu.SemaphoreType.DMA((pairs,)),
        ],
        compiler_params=pltpu.CompilerParams(vmem_limit_bytes=VMEM_LIMIT),
        cost_estimate=pl.CostEstimate(flops=1, bytes_accessed=1, transcendentals=0),
    )(me1, jt, r)


def front(order, me1, gauge_count, gauge_offset, gauge_resid, feats, half, own):
    depth, params = feats.shape
    cap = gauge_offset.size // 2
    panel = params // STRIDE
    trail = params - panel
    hbm = pl.BlockSpec(memory_space=pl.ANY)
    return pl.pallas_call(
        functools.partial(front_kernel, order),
        out_shape=[f32(half + 1, own, panel)] * 2 + [bf16(trail, cap), bf16(16, cap)],
        in_specs=[SMEM_SPEC, SMEM_SPEC, VMEM_SPEC, VMEM_SPEC, hbm],
        out_specs=[hbm, hbm, hbm, VMEM_SPEC],
        scratch_shapes=[
            pltpu.VMEM((depth, params), jnp.bfloat16),
            pltpu.VMEM((panel, cap), jnp.bfloat16),
            pltpu.VMEM((trail, cap), jnp.bfloat16),
            pltpu.VMEM((trail, panel), jnp.float32),
            pltpu.VMEM((panel, panel), jnp.float32),
            pltpu.VMEM((2, own, panel), jnp.float32),
            pltpu.SemaphoreType.DMA((params // BLK,)),
            pltpu.SemaphoreType.DMA((2,)),
            pltpu.SemaphoreType.DMA((2, half + 1)),
        ],
        compiler_params=pltpu.CompilerParams(vmem_limit_bytes=VMEM_LIMIT),
        cost_estimate=pl.CostEstimate(flops=1, bytes_accessed=1, transcendentals=0),
    )(me1, gauge_count, gauge_offset, gauge_resid, feats)


def swap(x, axis, bit):
    n = lax.axis_size(axis)
    return lax.ppermute(x, axis, [(i, i ^ (1 << bit)) for i in range(n)])


def panel_fold_kernel(bit, me_ref, kept_ref, got_ref, sent_out, kept_out):
    mine = (me_ref[0] >> bit) & 1
    size = kept_out.shape[0] - 1
    for k in range(size):
        sent_out[k] = kept_ref[(1 - mine) * size + k] + got_ref[(1 - mine) * size + k]
        kept_out[k] = kept_ref[mine * size + k] + got_ref[mine * size + k]
    total = kept_ref[2 * size] + got_ref[2 * size]
    sent_out[size] = total
    kept_out[size] = total


def fold(kept, got, me, bit):
    mine = (me >> bit) & 1
    size = kept.shape[0] // 2
    kept = kept.reshape((2, size) + kept.shape[1:])
    got = got.reshape(kept.shape)

    def part(which):
        return lax.dynamic_index_in_dim(kept, which, 0, False) + lax.dynamic_index_in_dim(got, which, 0, False)

    return part(1 - mine), part(mine)


def mirror(sums, own, ks, row, others):
    flat = [x for pair in sums for x in pair]
    widths = [pair[0].shape[-1] for pair in sums]
    new = [len(pair) == 2 for pair in sums]
    total = sum(widths)

    def kernel(*refs):
        ins, outs = list(refs[: len(flat)]), list(refs[len(flat) + len(others) :])
        turned_ref = outs.pop()
        at = 0
        for wide, pair in zip(widths, new):
            x = ins.pop(0)
            x = x[0] + ins.pop(0)[0] if pair else x[...]
            if pair:
                outs.pop(0)[...] = x
            turned_ref[at : at + wide, :] = x.T
            at += wide
        if others:
            outs.pop(0)[...] = jnp.concatenate([x[...] for x in reversed(refs[len(flat) : len(flat) + len(others)])], axis=1)
        for k in ks:
            outs.pop(0)[...] = turned_ref[k * own : (k + 1) * own, :]
        if row:
            outs.pop(0)[...] = turned_ref[row : row + 8, :]

    shapes = [f32(own, w) for w, pair in zip(widths, new) if pair] + [f32(own, own * len(others))] * bool(others)
    first = len(shapes)
    shapes += [f32(own, own)] * len(ks) + [f32(8, own)] * bool(row)
    out = list(call(kernel, flat + others, shapes, [pltpu.VMEM((total, own), jnp.float32)]))
    return out[:first], out[first : first + len(ks)], out[-1]


def factor_block(a):
    size = a.shape[0]
    shape = (8, size)
    lane = lax.broadcasted_iota(jnp.int32, shape, 1)
    sub = lax.broadcasted_iota(jnp.int32, shape, 0)
    groups = [a[at : at + 8] for at in range(0, size, 8)]

    def column(x, j):
        return jnp.broadcast_to(x[:, j : j + 1], shape)

    def row(x, s):
        return jnp.broadcast_to(x[s : s + 1, :], shape)

    uppers, lowers = [], []
    for g, x in enumerate(groups):
        first = 8 * g
        inside = (lane >= first) & (lane < first + 8)
        columns = [column(x, first + k) for k in range(8)]
        pivots = jnp.zeros(shape, jnp.float32)
        inverses, rows, cross = [], [], {}
        for k in range(8):
            pivot = row(columns[k], k)
            inverse = pltpu.reciprocal(pivot, approx=True)
            inverse = inverse * (2.0 - pivot * inverse)
            scaled = columns[k] * inverse
            for m in range(k + 1, 8):
                cross[k, m] = row(columns[m], k)
                columns[m] = columns[m] - scaled * cross[k, m]
            at = lane == first + k
            this = jnp.where(at, 1.0, row(x, k))
            x = jnp.where(at & (sub >= k), jnp.where(sub == k, 1.0, 0.0), x) - jnp.where(sub > k, scaled, 0.0) * this
            pivots = jnp.where(sub == k, pivot, pivots)
            inverses.append(inverse)
            rows.append(jnp.where(inside & (lane > first + k), 0.0, this))
        for h in range(g + 1, len(groups)):
            below = groups[h]
            columns = [column(below, first + k) for k in range(8)]
            below = jnp.where(inside, 0.0, below)
            for k in range(8):
                scaled = columns[k] * inverses[k]
                for m in range(k + 1, 8):
                    columns[m] = columns[m] - scaled * cross[k, m]
                below = below - scaled * rows[k]
            groups[h] = below
        root = lax.rsqrt(pivots)
        root = root * (1.5 - 0.5 * pivots * root * root)
        scaled = x * root
        off = lane - first - sub
        uppers.append(jnp.where(off > 0, scaled, jnp.where(off == 0, pivots * root, 0.0)))
        lowers.append(jnp.where(off <= 0, scaled, 0.0))
    return jnp.concatenate(uppers, axis=0).T, jnp.concatenate(lowers, axis=0)


def factor_first_kernel(me_ref, mine_ref, other_ref, damp_ref, g_ref, l11_ref, i11_ref, l21_ref, rest_ref):
    core = me_ref[0] & 1
    half = l11_ref.shape[0]
    rows = half // 2
    mine, other = mine_ref[0], other_ref[0]
    low, high = jnp.where(core == 0, mine, other), jnp.where(core == 0, other, mine)

    def opened(x):
        return jnp.concatenate([x[:, :half], x[:, half:]], axis=0)

    row = lax.broadcasted_iota(jnp.int32, (half, half), 0)
    col = lax.broadcasted_iota(jnp.int32, (half, half), 1)
    n11 = opened(low[:rows]) + jnp.where(row == col, damp_ref[:half, 0:1], 0.0)
    n22 = opened(high[:rows]) + jnp.where(row == col, damp_ref[half:, 0:1], 0.0)
    n21 = jnp.concatenate([opened(x[rows : rows + rows // 2]) for x in (low, high)], axis=0)
    g_ref[...] = mine[rows + rows // 2 : rows + rows // 2 + 8]
    l11, i11 = factor_block(n11)
    l21 = dot_nt(n21, i11, EXACT)
    l11_ref[...] = l11
    i11_ref[...] = i11
    l21_ref[...] = l21
    rest_ref[...] = n22 - dot_nt(l21, l21, EXACT)


def factor_second_kernel(l11_ref, i11_ref, l21_ref, rest_ref, factor_ref, inverse_ref):
    half = l11_ref.shape[0]
    l22, i22 = factor_block(rest_ref[...])
    before = jnp.dot(l21_ref[...], i11_ref[...], precision=EXACT, preferred_element_type=jnp.float32)
    zero = jnp.zeros((half, half), jnp.float32)
    factor_ref[:half, :half] = l11_ref[...]
    factor_ref[:half, half:] = zero
    factor_ref[half:, :half] = l21_ref[...]
    factor_ref[half:, half:] = l22
    inverse_ref[:half, :half] = i11_ref[...]
    inverse_ref[:half, half:] = zero
    inverse_ref[half:, :half] = -jnp.dot(i22, before, precision=EXACT, preferred_element_type=jnp.float32)
    inverse_ref[half:, half:] = i22


def lower_kernel(inverse_ref, g1_ref, held_ref, lower_ref, out_ref, y_ref, flat_ref):
    inverse = inverse_ref[...]
    count, own, size = held_ref.shape
    lower = dot_nt(held_ref[...].reshape(count * own, size), inverse, EXACT).reshape(count, own, size)
    lower_ref[...] = lower
    out_ref[...] = lower[0]
    y = dot_nt(g1_ref[...], inverse, EXACT)
    y_ref[...] = y
    flat_ref[...] = y[0]


def product_kernel(bits, me_ref, mine_ref, other_ref, product_ref, all_ref):
    me = me_ref[0]
    own = product_ref.shape[0]
    for k in range(mine_ref.shape[0]):
        owner = me ^ sum(((k >> i) & 1) << bit for i, bit in enumerate(bits))
        all_ref[pl.ds(pl.multiple_of(owner * own, 16), own), :] = mine_ref[k]
        all_ref[pl.ds(pl.multiple_of((owner ^ 1) * own, 16), own), :] = other_ref[k]
    product_ref[...] = dot_nt(mine_ref[0], all_ref[...], EXACT)


def last_kernel(n_chunks, me_ref, damp_ref, product_ref, g2_ref, y_ref, lower_ref, *refs):
    chunks, mirrors, (schur_ref, rhs_ref) = refs[:n_chunks], refs[n_chunks:-2], refs[-2:]
    rhs_ref[...] = (g2_ref[...] - dot_nt(y_ref[...], lower_ref[...], EXACT))[0]
    me = me_ref[0]
    own = schur_ref.shape[0]
    turned = [m[...] for m in reversed(mirrors[1:])] + [mirrors[0][...]]
    width = schur_ref.shape[1] - sum(x.shape[1] for x in turned)
    whole = jnp.concatenate([c[...] for c in chunks], axis=1)[:, :width]
    row = lax.broadcasted_iota(jnp.int32, (own, own), 0)
    col = lax.broadcasted_iota(jnp.int32, (own, own), 1)
    nat = own * STRIDE // (STRIDE - 1)
    target = lax.broadcasted_iota(jnp.int32, (own, nat), 0)
    target = target + 1 + ((target * 9363) >> 16)
    pick = target == lax.broadcasted_iota(jnp.int32, (own, nat), 1)
    damp = jnp.sum(jnp.where(pick, damp_ref[pl.ds(me, 1), :], 0.0), axis=1, keepdims=True)
    first = whole[:, :own] + jnp.where(row == col, damp, 0.0)
    whole = jnp.concatenate([first, whole[:, own:]] + turned, axis=1)
    schur_ref[...] = pltpu.roll(whole, me * own, 1) - product_ref[...]


def per_device(features, gauge_offset, gauge_count, gauge_resid, damping):
    tiles_here, samples, params = features.shape
    slots = gauge_offset.shape[1]
    axis = "tile"
    n = lax.axis_size(axis)
    panel = params // STRIDE
    trail = params - panel
    own = trail // n
    if n != 16 or own != 112 or params % BLK:
        return per_device_plain(features, gauge_offset, gauge_count, gauge_resid, damping)
    count = n // 2 - 1
    half = n // 2
    widths = (384, 384, 256)
    me = lax.axis_index(axis)
    me1 = me.astype(jnp.int32).reshape(1)
    order = [1, 2, 3]
    orders = [order] * len(widths)
    last = [()]

    def then(*xs):
        xs, last[0] = lax.optimization_barrier((xs, last[0]))
        return xs

    def did(x):
        last[0] = x
        return x

    feats = features.reshape(tiles_here * samples, params)
    sent, p, jt, r = did(front(order, me1, gauge_count, gauge_offset, gauge_resid, feats, half, own))
    p_got = swap(sent, axis, 0)

    def panel_fold(p, got, bit):
        shape = f32(p.shape[0] // 2 + 1, *p.shape[1:])
        sent, p = did(call(functools.partial(panel_fold_kernel, bit), then(me1, p, got), [shape] * 2))
        return p, swap(sent, axis, bit)

    def trail_fold(q, step):
        bit = orders[q][step]
        sent, t[q] = did(fold(*then(t[q], t_got[q]), me, bit))
        t_sent[q] = sent

    def trail_send(q, step):
        t_got[q] = swap(t_sent[q], axis, orders[q][step])

    def trail_step(q, step):
        trail_fold(q, step)
        trail_send(q, step)

    def trail_sum(q):
        kept, got = then(t[q], t_got[q])
        return did(kept[0] + got[0])

    def joined(held, got):
        return did(jnp.concatenate(then(held, got), axis=0))

    p, p_got = panel_fold(p, p_got, order[0])
    out = did(trailing(*then(me1, jt, r), orders, half, own, widths))
    t_sent, t = out[: len(widths)], list(out[len(widths) :])
    t_sent, p_got = lax.optimization_barrier((t_sent, p_got))
    t_got = [swap(t_sent[0], axis, 0)]
    p, p_got = panel_fold(p, p_got, order[1])
    t_sent = list(lax.optimization_barrier((t_sent, p))[0])
    t_got += [swap(x, axis, 0) for x in t_sent[1:]]
    trail_step(0, 0)
    p, p_got = panel_fold(p, p_got, order[2])
    trail_step(1, 0)
    trail_step(2, 0)
    damp_panel, damp_trail = then(damping)[0].reshape(panel, STRIDE), damping.reshape(n, params // n)
    damp_panel = did(damp_panel)
    p, p_got = then(p, p_got)
    p = did(p + p_got)
    held, n11 = p[:1], p[1:]
    n11_got = swap(n11, axis, 0)
    got = swap(held, axis, order[2])
    trail_step(0, 1)
    g1, *state = did(
        call(factor_first_kernel, then(me1, n11, n11_got, damp_panel), [f32(8, panel)] + [f32(panel // 2, panel // 2)] * 4)
    )
    held = joined(held, got)
    got = swap(held, axis, order[1])
    trail_step(0, 2)
    trail_step(1, 1)
    held = joined(held, got)
    got = swap(held, axis, order[0])
    trail_step(2, 1)
    factor, inverse = did(call(factor_second_kernel, then(*state), [f32(panel, panel)] * 2))
    trail_step(1, 2)
    first = trail_sum(0)
    near = widths[0] // own
    _, blocks, _ = did(mirror([then(first)], own, range(1, near), 0, []))

    def mirrored(blocks, ks):
        return [lax.ppermute(b, axis, [(i, (i + k) % n) for i in range(n)]) for k, b in zip(ks, blocks)]

    near_mirrors = mirrored(blocks, range(1, near))
    trail_step(2, 2)
    held = joined(held, got)
    mine, lower, y, y0 = did(
        call(lower_kernel, then(inverse, g1, held), [f32(half, own, panel), f32(own, panel), f32(8, panel), f32(panel)])
    )
    second = trail_sum(1)
    (third, right), blocks, g2 = did(
        mirror([(first,), (second,), then(t[2], t_got[2])], own, range(near, count + 1), (count + 2) * own, near_mirrors)
    )
    chunks = [first, second, third]
    mirrors = mirrored(blocks, range(near, count + 1))
    other = swap(lax.optimization_barrier((mine, chunks))[0], axis, 0)
    product = did(
        call(
            functools.partial(product_kernel, list(reversed(order))),
            then(me1, mine, other),
            f32(own, trail),
            [pltpu.VMEM((trail, panel), jnp.float32)],
        )
    )
    schur, rhs0 = call(
        functools.partial(last_kernel, len(widths)),
        then(me1, damp_trail, product, g2, y, lower, *chunks, right, *mirrors),
        [f32(own, trail), f32(own)],
    )
    return (factor, lower, schur, y0, rhs0)


def per_device_plain(features, gauge_offset, gauge_count, gauge_resid, damping):
    tiles_here, samples, params = features.shape
    slots = gauge_offset.shape[1]
    panel = params // 8
    trail = params - panel
    rows_here = tiles_here * slots
    slot_ids = lax.broadcasted_iota(jnp.int32, (tiles_here, slots), 1)
    live = slot_ids < gauge_count[:, None]
    sample_ids = lax.broadcasted_iota(jnp.int32, (tiles_here, slots, samples), 2)
    starts = gauge_offset[:, :, None]
    inside = (sample_ids >= starts) & (sample_ids < starts + LWIN) & live[:, :, None]
    window = jnp.where(inside, 1.0 / LWIN, 0.0).astype(jnp.bfloat16)
    jac = jnp.einsum("tgw,twp->tgp", window, features, preferred_element_type=jnp.float32)
    jac = jac.astype(jnp.bfloat16).reshape(rows_here, params)
    resid = jnp.where(live, gauge_resid, jnp.zeros_like(gauge_resid)).reshape(rows_here)
    grad_local = jnp.dot(resid, jac, preferred_element_type=jnp.float32)
    width = lax.axis_size("tile")
    owned = params // width
    owned_trail = owned - owned // 8
    index = lax.axis_index("tile")
    gauges = jac.shape[0]
    jac_split = jac.reshape(gauges, panel, 8)
    jac_panel = jac_split[:, :, 0]
    jac_trail = jac_split[:, :, 1:].reshape(gauges, trail)
    panel_local = lax.dot_general(jac, jac_panel, (((0,), (0,)), ((), ())), preferred_element_type=jnp.float32)
    panel_all, grad = lax.psum((panel_local, grad_local), "tile")
    own_trail = lax.psum_scatter(
        lax.dot_general(jac_trail, jac_trail, (((0,), (0,)), ((), ())), preferred_element_type=jnp.float32),
        "tile",
        scatter_dimension=0,
        tiled=True,
    )
    damp_split = damping.reshape(panel, 8)
    damp_trail = damp_split[:, 1:].reshape(trail)
    trail_ids = index * owned_trail + lax.broadcasted_iota(jnp.int32, (owned_trail, trail), 0)
    column_ids = lax.broadcasted_iota(jnp.int32, (owned_trail, trail), 1)
    own_trail = own_trail + jnp.where(trail_ids == column_ids, damp_trail[None, :], 0.0)
    panel_split = panel_all.reshape(panel, 8, panel)
    n11 = panel_split[:, 0, :] + jnp.diag(damp_split[:, 0])
    n21 = panel_split[:, 1:, :].reshape(trail, panel)
    panel_factor = jnp.linalg.cholesky(n11)
    lower_all = lax.linalg.triangular_solve(panel_factor, n21, left_side=False, lower=True, transpose_a=True)
    lower_own = lax.dynamic_slice_in_dim(lower_all, index * owned_trail, owned_trail, 0)
    schur = own_trail - jnp.dot(lower_own, lower_all.T, precision=lax.Precision.HIGHEST)
    grad_split = grad.reshape(panel, 8)
    first_part = grad_split[:, 0]
    second_part = grad_split[:, 1:].reshape(trail)
    panel_rhs = lax.linalg.triangular_solve(panel_factor, first_part[:, None], left_side=True, lower=True)[:, 0]
    second_own = lax.dynamic_slice_in_dim(second_part, index * owned_trail, owned_trail, 0)
    trail_rhs = second_own - jnp.dot(lower_own, panel_rhs, precision=lax.Precision.HIGHEST)
    return (panel_factor, lower_own, schur, panel_rhs, trail_rhs)


def solution(mesh):
    return jax.shard_map(
        per_device,
        mesh=mesh,
        in_specs=(
            P(("groups", "tile"), None, None),
            P(("groups", "tile"), None),
            P(("groups", "tile")),
            P(("groups", "tile"), None),
            P("groups"),
        ),
        out_specs=(
            P("groups", None),
            P(("groups", "tile"), None),
            P(("groups", "tile"), None),
            P("groups"),
            P(("groups", "tile")),
        ),
        check_vma=False,
    )
```
